256 devices in a mesh: seq: 64 (over y, z_hi, x, core), head: 4 (over z_lo).
Axes of the slice: x: 4, y: 4, z: 8 (z_hi: 2, z_lo: 4; z = z_hi * 4 + z_lo), core: 2. Of those that a mesh axis runs over, the one named last changes fastest.
Arguments:
- queries: bfloat16 [24576, 3072], P('seq', 'head'), may hold values from -18 to 18
- key_states: bfloat16 [24576, 3072], P('seq', 'head'), may hold values from -6 to 6
- value_states: bfloat16 [24576, 3072], P('seq', 'head'), may hold values from -6 to 6
- out_weight: bfloat16 [3072, 3072], P('head'), may hold values from -0.15625 to 0.15625
Outputs:
- mixed: bfloat16 [24576, 3072], P('seq', 'head')
The draws below stay inside these ranges and needn't reach their ends.
All inputs are finite; a program needn't handle non-finite values.
Results may differ from the reference program's by a relative error of at most 0.023.
Values may be sent and summed in bfloat16 or wider, within the bound.
No kernel may reach another device: no remote copies, remote signals or barrier semaphores. Data moves between devices by JAX's collectives and lax.ppermute only.
A program may use at most 64 MiB of HBM per device.

```python
import jax
import jax.numpy as jnp
from jax import lax

HEADS = 24
HD = 128
D = 3072
SPAN = 384
TOKENS = 24576
WIDTH = 3072


def draw_key_states(key, part):
    key = jax.random.fold_in(key, 11)
    fresh = jax.random.normal(key, (TOKENS, HEADS * HD), jnp.float32)
    return jnp.clip(fresh, -6.0, 6.0).astype(jnp.bfloat16)


def draw_queries(key, part):
    key = jax.random.fold_in(key, 23)
    fresh = jax.random.normal(key, (TOKENS, HEADS * HD), jnp.float32)
    return jnp.clip(fresh, -6.0, 6.0).astype(jnp.bfloat16)


def spiked(values, key, source, target, parts, factor):
    def block_of(position):
        return (jnp.arange(values.shape[position]) // (values.shape[position] // parts)).reshape((-1,) + (1,) * (values.ndim - 1 - position))

    first = jax.random.permutation(key, parts)[block_of(target)]
    far = (block_of(target) + parts // 2) % parts
    return jnp.where((block_of(source) == first) | (block_of(source) == far), factor * values, values)


def level_of(rng, dims, split, least, top_value):
    def one(dim, blocks):
        heights = jax.random.uniform(jax.random.fold_in(jax.random.fold_in(rng, 6), dim), (blocks,), jnp.float32, least / len(split), top_value / len(split))
        return jnp.repeat(jnp.exp(heights), dims[dim] // blocks).reshape((-1,) + (1,) * (len(dims) - dim - 1))

    gain = one(*split[0])
    for cut in split[1:]:
        gain = gain * one(*cut)
    return gain


def scatter_about(own_key, shape, scale, limit, shards=(), kind=jnp.bfloat16):
    array = jax.random.normal(own_key, shape, jnp.float32) * scale
    if len(shards) > 0:
        array = level_of(own_key, shape, shards, -0.22, 0.18) * array
    return jnp.clip(array, min=-limit, max=limit).astype(kind)


def heavy_noise(own_key, extent, deviation, reach, shards, heavy, kind=jnp.bfloat16):
    values = deviation * jax.random.normal(own_key, extent, jnp.float32)
    if shards:
        values = values * level_of(own_key, extent, shards, -0.22, 0.18)
    return jnp.clip(spiked(values, jax.random.fold_in(own_key, 3), *heavy), -reach, reach).astype(kind)


def setup_inputs(seed: int = 0) -> dict:
    seeds = jax.random.split(jax.random.key(seed), 5)
    queries = draw_queries(jax.random.fold_in(seeds[4], 71), 0)
    key_states = draw_key_states(jax.random.fold_in(seeds[4], 71), 0)
    value_states = scatter_about(seeds[2], (TOKENS, WIDTH), 1.0, 6.0, ((0, 64), (1, 4)))
    out_weight = heavy_noise(seeds[3], (WIDTH, D), WIDTH ** -0.5, 0.15625, ((0, 4),), (0, 1, 4, 2.0))
    return dict(queries=queries, key_states=key_states, value_states=value_states, out_weight=out_weight)


NEG_FILL = -1e30


def reference(queries, key_states, value_states, out_weight):
    spans = TOKENS // SPAN
    query_split = queries.reshape(spans, SPAN, HEADS, HD)
    padding = jnp.zeros((2 * SPAN, HEADS * HD), jnp.bfloat16)
    key_padded = jnp.concatenate([padding, key_states, padding], axis=0).reshape(-1, HEADS, HD)
    value_padded = jnp.concatenate([padding, value_states, padding], axis=0).reshape(-1, HEADS, HD)
    band_offset = (jnp.arange(5 * SPAN, dtype=jnp.int32) // SPAN - 2).astype(jnp.int32)

    def attend(span_pos):
        query_block = query_split[span_pos].astype(jnp.float32)
        first_row = (span_pos * SPAN).astype(jnp.int32)
        key_block = lax.dynamic_slice_in_dim(key_padded, first_row, 5 * SPAN, 0).astype(jnp.float32)
        value_block = lax.dynamic_slice_in_dim(value_padded, first_row, 5 * SPAN, 0).astype(jnp.float32)
        inside = (span_pos + band_offset >= 0) & (span_pos + band_offset < spans)
        scores = jnp.einsum('qhd,khd->hqk', query_block, key_block) * (HD ** -0.5)
        scores = jnp.where(inside[None, None, :], scores, NEG_FILL)
        row_max = jnp.max(scores, axis=2)
        weights = jnp.exp(scores - row_max[:, :, None])
        weights = jnp.where(inside[None, None, :], weights, 0.0)
        row_sum = jnp.sum(weights, axis=2)
        rounded = lax.optimization_barrier(weights.astype(jnp.bfloat16)).astype(jnp.float32)
        summed = jnp.einsum('hqk,khd->hqd', rounded, value_block)
        result = summed / row_sum[:, :, None]
        return jnp.transpose(result, (1, 0, 2)).reshape(SPAN, HEADS * HD).astype(jnp.bfloat16)

    attended = lax.map(attend, jnp.arange(spans, dtype=jnp.int32)).reshape(TOKENS, HEADS * HD)
    return jnp.dot(attended, out_weight, preferred_element_type=jnp.float32).astype(jnp.bfloat16)
```

```python
import functools
import math

import jax
import jax.numpy as jnp
from jax import lax
from jax.experimental import pallas as pl
from jax.experimental.pallas import tpu as pltpu
from jax.sharding import PartitionSpec as P

HD = 128
SPANS = 64
HEAD_PEERS = 4
CHUNK = 2
SCALE = math.log2(math.e) / math.sqrt(HD)
LOWEST = -1e30


def scores_of(query, key):
    return lax.dot_general(query, key, (((1,), (1,)), ((), ())), preferred_element_type=jnp.float32)


def with_ones(value):
    return jnp.concatenate([value, jnp.ones_like(value)], axis=1)


def widen(column, times):
    return jnp.concatenate([column] * times, axis=1)


def weights_of(scores, shift):
    return jnp.exp2(scores * SCALE - widen(shift, scores.shape[1] // HD)).astype(jnp.bfloat16)


def lanes(h):
    return slice(h * HD, (h + 1) * HD)


def near_kernel(q_ref, k_ref, v_ref, pk_ref, pv_ref, acc_ref, max_ref):
    rows = q_ref.shape[0]
    for h in range(q_ref.shape[1] // HD):
        at = lanes(h)
        query = q_ref[:, at]
        s0 = scores_of(query, k_ref[:, at])
        s1 = scores_of(query, pk_ref[:, at])
        top = jnp.maximum(jnp.max(s0, axis=1, keepdims=True), jnp.max(s1, axis=1, keepdims=True))
        top = jnp.broadcast_to(top, (rows, HD))
        shift = top * SCALE
        acc_ref[h] = jnp.dot(
            weights_of(s0, shift), with_ones(v_ref[:, at]), preferred_element_type=jnp.float32
        ) + jnp.dot(
            weights_of(s1, shift), with_ones(pv_ref[:, at]), preferred_element_type=jnp.float32
        )
        max_ref[h] = top


def far_kernel(first, valid_ref, q_ref, acc_ref, max_ref, *refs):
    *blocks, out_ref = refs
    rows = q_ref.shape[0]
    half = CHUNK * HD
    for i in range(CHUNK):
        h = first + i
        query = q_ref[:, lanes(h)]
        old = max_ref[h]
        scores = []
        top = old
        for b, ref in enumerate(blocks):
            s = scores_of(query, ref[:, lanes(i)])
            peak = jnp.broadcast_to(jnp.max(s, axis=1, keepdims=True), (rows, HD))
            top = jnp.maximum(top, jnp.where(valid_ref[b] > 0, peak, LOWEST))
            scores.append(s)
        shift = top * SCALE
        total = acc_ref[h] * widen(jnp.exp2(old * SCALE - shift), 2)
        for b, ref in enumerate(blocks):
            used = jnp.where(valid_ref[b] > 0, shift, -LOWEST)
            total += jnp.dot(
                weights_of(scores[b], used),
                with_ones(ref[:, half + i * HD : half + (i + 1) * HD]),
                preferred_element_type=jnp.float32,
            )
        out_ref[:, lanes(i)] = (total[:, :HD] / total[:, HD:]).astype(out_ref.dtype)


def in_vmem(count):
    return [pl.BlockSpec(memory_space=pltpu.VMEM)] * count


def near_part(q, k, v, pk, pv):
    rows, width = q.shape
    heads = width // HD
    return pl.pallas_call(
        near_kernel,
        out_shape=(
            jax.ShapeDtypeStruct((heads, rows, 2 * HD), jnp.float32),
            jax.ShapeDtypeStruct((heads, rows, HD), jnp.float32),
        ),
        in_specs=in_vmem(5),
        out_specs=tuple(in_vmem(2)),
        compiler_params=pltpu.CompilerParams(vmem_limit_bytes=32 * 2**20),
        cost_estimate=pl.CostEstimate(
            flops=12 * heads * rows * rows * HD,
            bytes_accessed=10 * rows * width,
            transcendentals=2 * heads * rows * rows,
        ),
        name="near",
    )(q, k, v, pk, pv)


def far_part(first, valid, q, acc, top, blocks):
    rows = q.shape[0]
    return pl.pallas_call(
        functools.partial(far_kernel, first),
        out_shape=jax.ShapeDtypeStruct((rows, CHUNK * HD), jnp.bfloat16),
        in_specs=[pl.BlockSpec(memory_space=pltpu.SMEM)] + in_vmem(3 + len(blocks)),
        out_specs=pl.BlockSpec(memory_space=pltpu.VMEM),
        compiler_params=pltpu.CompilerParams(vmem_limit_bytes=32 * 2**20),
        cost_estimate=pl.CostEstimate(
            flops=6 * len(blocks) * CHUNK * rows * rows * HD,
            bytes_accessed=10 * rows * CHUNK * HD,
            transcendentals=len(blocks) * CHUNK * rows * rows,
        ),
        name=f"far{first}",
    )(valid, q, acc, top, *blocks)


def seq_pairs(step_of):
    return [(s, s + step_of(s)) for s in range(SPANS) if 0 <= s + step_of(s) < SPANS]


PAIR = seq_pairs(lambda s: 1 if s % 2 == 0 else -1)
SHARED = seq_pairs(lambda s: -2 if s % 2 == 0 else 2)
SINGLE = seq_pairs(lambda s: 2 if s % 2 == 0 else -2)


def body(queries, key_states, value_states, out_weight):
    rows, width = queries.shape
    heads = width // HD
    place = lax.axis_index("seq")
    even = place % 2 == 0
    has_after2, has_before2 = place + 2 < SPANS, place >= 2
    shared_ok = jnp.where(even, has_after2, has_before2)
    single_ok = jnp.where(even, has_before2, has_after2)
    swapped_ok = jnp.where(even, place >= 1, place + 1 < SPANS)
    valid = jnp.stack([shared_ok, single_ok, swapped_ok]).astype(jnp.int32)

    pair_key = lax.ppermute(key_states, "seq", PAIR)
    pair_value = lax.ppermute(value_states, "seq", PAIR)
    step = CHUNK * HD
    packed = [
        jnp.concatenate([key_states[:, a : a + step], value_states[:, a : a + step]], axis=1)
        for a in range(0, width, step)
    ]
    shared, single, swapped = [], [], []
    for chunk in packed:
        shared.append(lax.ppermute(chunk, "seq", SHARED))
        single.append(lax.ppermute(chunk, "seq", SINGLE))
    for chunk in shared:
        swapped.append(lax.ppermute(chunk, "seq", PAIR))

    acc, top = near_part(queries, key_states, value_states, pair_key, pair_value)
    attended = [
        far_part(i * CHUNK, valid, queries, acc, top, [shared[i], single[i], swapped[i]])
        for i in range(heads // CHUNK)
    ]
    return projected(jnp.concatenate(attended, axis=1), out_weight)


def projected(attended, out_weight):
    z = lax.axis_index("head")
    cols = out_weight.shape[1] // HEAD_PEERS
    low = z < 2
    half = attended.shape[0] // 2

    def term(part, which):
        weight = lax.dynamic_slice_in_dim(out_weight, which * cols, cols, 1)
        return jnp.dot(part, weight, preferred_element_type=jnp.float32)

    ends_in = [(0, 1), (3, 2)]
    across = [(1, 2), (2, 1)]
    outward = [(1, 0), (2, 3)]

    def sent(value, pairs):
        return lax.ppermute(value.astype(jnp.bfloat16), "head", pairs)

    outs = []
    for r in range(2):
        part = attended[r * half : (r + 1) * half]
        far = term(part, jnp.where(low, 3, 0))
        mid = term(part, jnp.where(low, 2, 1))
        beside = term(part, z ^ 1)
        own = term(part, z)
        far_in = sent(far, ends_in)
        mid_in = sent(mid, ends_in)
        beside_in = sent(beside, ends_in)
        crossed_far = sent(far + far_in, across)
        crossed_mid = sent(mid + mid_in, across)
        out_in = sent(beside + crossed_far, outward)
        outs.append((own + out_in + beside_in + crossed_mid).astype(jnp.bfloat16))
    return jnp.concatenate(outs, axis=0)


def solution(mesh):
    placed = (P("seq", "head"), P("seq", "head"), P("seq", "head"), P("head", None))
    return jax.shard_map(
        body, mesh=mesh, in_specs=placed, out_specs=P("seq", "head"), check_vma=False
    )
```

```python
import functools
import math

import jax
import jax.numpy as jnp
from jax import lax
from jax.experimental import pallas as pl
from jax.experimental.pallas import tpu as pltpu
from jax.sharding import PartitionSpec as P

HD = 128
SPANS = 64
HEAD_PEERS = 4
ROW = 8
DIRECT = 4
WEIGHT = 30
SCALE = math.log2(math.e) / math.sqrt(HD)
LOWEST = -1e30


def scores_of(query, key):
    return lax.dot_general(query, key, (((1,), (1,)), ((), ())), preferred_element_type=jnp.float32)


def with_ones(value):
    return jnp.concatenate([value, jnp.ones_like(value)], axis=1)


def widen(column, times):
    return jnp.concatenate([column] * times, axis=1)


def weights_of(scores, shift):
    return jnp.exp2(scores * SCALE - widen(shift, scores.shape[1] // HD)).astype(jnp.bfloat16)


def inverse(x):
    guess = pl.reciprocal(x, approx=True)
    return guess * (2.0 - x * guess)


def lanes(h):
    return slice(h * HD, (h + 1) * HD)


def near_kernel(q_ref, k_ref, v_ref, pk_ref, pv_ref, state_ref):
    rows = q_ref.shape[0]
    for h in range(q_ref.shape[1] // HD):
        at = lanes(h)
        query = q_ref[:, at]
        s0 = scores_of(query, k_ref[:, at])
        s1 = scores_of(query, pk_ref[:, at])
        top = jnp.maximum(jnp.max(s0, axis=1, keepdims=True), jnp.max(s1, axis=1, keepdims=True))
        top = jnp.broadcast_to(top, (rows, HD))
        shift = top * SCALE
        state_ref[h, :, : 2 * HD] = jnp.dot(
            weights_of(s0, shift), with_ones(v_ref[:, at]), preferred_element_type=jnp.float32
        ) + jnp.dot(
            weights_of(s1, shift), with_ones(pv_ref[:, at]), preferred_element_type=jnp.float32
        )
        state_ref[h, :, 2 * HD :] = top


def far_kernel(first, counts, closes, valid_ref, q_ref, state_ref, *refs):
    *blocks, out_ref = refs
    half = blocks[0].shape[1] // 2
    groups, at = [], 0
    for count in counts:
        groups.append(blocks[at : at + count])
        at += count
    rows = q_ref.shape[0]

    def part(group, lane):
        value = group[0][:, lane]
        for ref in group[1:]:
            value = value + ref[:, lane]
        return value

    for i in range(half // HD):
        h = first + i
        query = q_ref[:, lanes(h)]
        held = h if state_ref.shape[0] > half // HD else i
        old = state_ref[held, :, 2 * HD :]
        before = state_ref[held, :, : 2 * HD]
        scores = []
        top = old
        for b, group in enumerate(groups):
            s = scores_of(query, part(group, lanes(i)))
            peak = jnp.broadcast_to(jnp.max(s, axis=1, keepdims=True), (rows, HD))
            top = jnp.maximum(top, jnp.where(valid_ref[b] > 0, peak, LOWEST))
            scores.append(s)
        shift = top * SCALE
        total = before * widen(jnp.exp2(old * SCALE - shift), 2)
        for b, group in enumerate(groups):
            used = jnp.where(valid_ref[b] > 0, shift, -LOWEST)
            value = part(group, slice(half + i * HD, half + (i + 1) * HD))
            total += jnp.dot(
                weights_of(scores[b], used), with_ones(value), preferred_element_type=jnp.float32
            )
        if closes:
            out_ref[:, lanes(i)] = (total[:, :HD] * inverse(total[:, HD:])).astype(out_ref.dtype)
        else:
            out_ref[i, :, : 2 * HD] = total
            out_ref[i, :, 2 * HD :] = top


def pack_kernel(cut, k_ref, v_ref, out_ref, sems):
    wide = out_ref.shape[1] // 2
    copies = [
        pltpu.make_async_copy(
            ref.at[:, pl.ds(cut, wide)], out_ref.at[:, pl.ds(i * wide, wide)], sems.at[i]
        )
        for i, ref in enumerate((k_ref, v_ref))
    ]
    for copy in copies:
        copy.start()
    for copy in copies:
        copy.wait()


def columns_kernel(which_ref, w_ref, *refs):
    *outs, sems = refs
    copies = []
    for i, out in enumerate(outs):
        cols = out.shape[1]
        at = pl.ds(pl.multiple_of(which_ref[i] * cols, cols), cols)
        copies.append(pltpu.make_async_copy(w_ref.at[:, at], out, sems.at[i]))
    for copy in copies:
        copy.start()
    for copy in copies:
        copy.wait()


def project_kernel(att0_ref, att1_ref, *refs):
    half = len(refs) // 2
    weights, outs = (refs[:1], refs[1:]) if len(refs) == 3 else (refs[:half], refs[half:])
    cut = att0_ref.shape[1]
    each = len(outs) // len(weights)
    for i, w_ref in enumerate(weights):
        for j in range(each):
            out_ref = outs[i * each + j]
            rows = out_ref.shape[0]
            at = slice(j * rows, (j + 1) * rows)
            out_ref[...] = (
                jnp.dot(att0_ref[at, :], w_ref[:cut, :], preferred_element_type=jnp.float32)
                + jnp.dot(att1_ref[at, :], w_ref[cut:, :], preferred_element_type=jnp.float32)
            ).astype(out_ref.dtype)


def last_sum_kernel(*refs):
    *parts, out_ref = refs
    out_ref[...] = sum(ref[...].astype(jnp.float32) for ref in parts).astype(out_ref.dtype)


def in_vmem(count):
    return [pl.BlockSpec(memory_space=pltpu.VMEM)] * count


def near_part(q, k, v, pk, pv):
    rows, width = q.shape
    heads = width // HD
    return pl.pallas_call(
        near_kernel,
        out_shape=jax.ShapeDtypeStruct((heads, rows, 3 * HD), jnp.float32),
        in_specs=in_vmem(5),
        out_specs=in_vmem(1)[0],
        compiler_params=pltpu.CompilerParams(vmem_limit_bytes=8 * 2**20),
        cost_estimate=pl.CostEstimate(
            flops=WEIGHT * 12 * heads * rows * rows * HD,
            bytes_accessed=10 * rows * width,
            transcendentals=2 * heads * rows * rows,
        ),
        name="near",
    )(q, k, v, pk, pv)


def far_part(first, closes, valid, q, state, blocks):
    rows = q.shape[0]
    arrays = [array for block in blocks for array in block]
    heads = arrays[0].shape[1] // 2 // HD
    if closes:
        shape = jax.ShapeDtypeStruct((rows, heads * HD), jnp.bfloat16)
    else:
        shape = jax.ShapeDtypeStruct((heads, rows, 3 * HD), jnp.float32)
    return pl.pallas_call(
        functools.partial(far_kernel, first, [len(block) for block in blocks], closes),
        out_shape=shape,
        in_specs=[pl.BlockSpec(memory_space=pltpu.SMEM)] + in_vmem(2 + len(arrays)),
        out_specs=in_vmem(1)[0],
        compiler_params=pltpu.CompilerParams(vmem_limit_bytes=8 * 2**20),
        cost_estimate=pl.CostEstimate(
            flops=6 * len(blocks) * heads * rows * rows * HD,
            bytes_accessed=10 * rows * heads * HD,
            transcendentals=len(blocks) * heads * rows * rows,
        ),
        name=f"far{first}_{len(blocks)}",
    )(valid, q, state, *arrays)


def packed(k, v, cut, heads):
    rows = k.shape[0]
    return pl.pallas_call(
        functools.partial(pack_kernel, cut * HD),
        out_shape=jax.ShapeDtypeStruct((rows, 2 * heads * HD), k.dtype),
        in_specs=[pl.BlockSpec(memory_space=pl.ANY)] * 2,
        out_specs=pl.BlockSpec(memory_space=pltpu.VMEM),
        scratch_shapes=[pltpu.SemaphoreType.DMA((2,))],
        compiler_params=pltpu.CompilerParams(vmem_limit_bytes=60 * 2**20),
        cost_estimate=pl.CostEstimate(
            flops=0, bytes_accessed=8 * rows * heads * HD, transcendentals=0
        ),
        name=f"pack{cut}",
    )(k, v)


def seq_pairs(step_of, among=lambda s: True):
    return [
        (s, s + step_of(s)) for s in range(SPANS) if 0 <= s + step_of(s) < SPANS and among(s)
    ]


def mate_step(s):
    return 2 if s // 2 % 2 == 0 else -2


def other_step(s):
    return -mate_step(s)


def is_end(s):
    return s % ROW < 2 or s % ROW >= ROW - 2


MATE = seq_pairs(mate_step)
OTHER = seq_pairs(other_step)
OTHER_IN_ROW = seq_pairs(other_step, lambda s: not is_end(s))
ONWARD = [
    (s + mate_step(s), s + other_step(s))
    for s in range(SPANS)
    if is_end(s) and 0 <= s + other_step(s) < SPANS
]
PAIR = seq_pairs(lambda s: 1 if s % 2 == 0 else -1)
MATE_SHARED = [(s, p) for s, p in PAIR if s % 2 == s // 2 % 2]
OTHER_SHARED = [(s, p) for s, p in PAIR if s % 2 != s // 2 % 2]


def body(queries, key_states, value_states, out_weight):
    place = lax.axis_index("seq")
    chip = place // 2
    mate_chip = chip ^ 1
    other_chip = 2 * chip - mate_chip
    third = jnp.where(place % 2 == 0, chip - 1, chip + 1)

    def inside(c):
        return (c >= 0) & (c < SPANS // 2)

    valid = jnp.stack([inside(mate_chip), inside(other_chip), inside(third)]).astype(jnp.int32)
    total_heads = key_states.shape[1] // HD

    pair_key = lax.ppermute(key_states, "seq", PAIR)
    pair_value = lax.ppermute(value_states, "seq", PAIR)
    direct = packed(key_states, value_states, 0, DIRECT)
    other0 = lax.ppermute(direct, "seq", OTHER)
    direct, keys, values = lax.optimization_barrier((direct, key_states, value_states))
    relayed = packed(keys, values, DIRECT, total_heads - DIRECT)
    mate1 = lax.ppermute(relayed, "seq", MATE)
    mate0 = lax.ppermute(direct, "seq", MATE)
    relayed, pair_key, pair_value = lax.optimization_barrier((relayed, pair_key, pair_value))
    row_other1 = lax.ppermute(relayed, "seq", OTHER_IN_ROW)

    z = lax.axis_index("head")
    weights = weight_columns(
        jnp.stack([z ^ 3, z ^ 1, z ^ 2, z]), out_weight
    )
    queries, mate1, *weights = lax.optimization_barrier((queries, mate1, *weights))
    passed_other1 = lax.ppermute(mate1, "seq", ONWARD)
    state = near_part(queries, key_states, value_states, pair_key, pair_value)
    other1 = row_other1 + passed_other1

    mate_shared0 = lax.ppermute(mate0, "seq", MATE_SHARED)
    mate_shared1 = lax.ppermute(mate1, "seq", MATE_SHARED)
    other_shared1 = lax.ppermute(other1, "seq", OTHER_SHARED)

    mate1, mate_shared1 = lax.optimization_barrier((mate1, mate_shared1))
    state1 = far_part(DIRECT, False, valid[:1], queries, state, [[mate1]])
    mate0, mate_shared0, state1 = lax.optimization_barrier((mate0, mate_shared0, state1))
    state0 = far_part(0, False, valid[:1], queries, state, [[mate0]])
    other0, state0, state1 = lax.optimization_barrier((other0, state0, state1))
    other_shared0 = lax.ppermute(other0, "seq", OTHER_SHARED)
    att1 = far_part(
        DIRECT, True, valid[1:], queries, state1, [[other1], [mate_shared1, other_shared1]]
    )
    state0 = far_part(0, False, valid[1:2], queries, state0, [[other0]])
    att0 = far_part(0, True, valid[2:], queries, state0, [[mate_shared0, other_shared0]])
    return projected(att0, att1, weights)


def small_call(kernel, name, out_shape, operands, scalars=(), in_hbm=(), sems=0, limit=8 * 2**20):
    return pl.pallas_call(
        kernel,
        out_shape=out_shape,
        in_specs=[pl.BlockSpec(memory_space=pltpu.SMEM)] * len(scalars)
        + [pl.BlockSpec(memory_space=pltpu.HBM)] * len(in_hbm)
        + in_vmem(len(operands)),
        out_specs=in_vmem(len(out_shape)),
        scratch_shapes=[pltpu.SemaphoreType.DMA((sems,))] if sems else [],
        compiler_params=pltpu.CompilerParams(vmem_limit_bytes=limit),
        cost_estimate=pl.CostEstimate(
            flops=0,
            bytes_accessed=2 * sum(o.size * o.dtype.itemsize for o in out_shape),
            transcendentals=0,
        ),
        name=name,
    )(*[x.astype(jnp.int32) for x in scalars], *in_hbm, *operands)


def weight_columns(which, out_weight):
    depth = out_weight.shape[0]
    cols = out_weight.shape[1] // HEAD_PEERS
    return small_call(
        columns_kernel,
        "columns",
        [jax.ShapeDtypeStruct((depth, cols), out_weight.dtype)] * HEAD_PEERS,
        (),
        scalars=(which,),
        in_hbm=(out_weight,),
        sems=HEAD_PEERS,
        limit=48 * 2**20,
    )


def projection(att0, att1, weights, pieces):
    rows = att0.shape[0]
    depth, cols = weights[0].shape
    count = len(weights)
    return pl.pallas_call(
        project_kernel,
        out_shape=[jax.ShapeDtypeStruct((rows // pieces, cols), jnp.bfloat16)] * (count * pieces),
        in_specs=in_vmem(2 + count),
        out_specs=in_vmem(count * pieces),
        compiler_params=pltpu.CompilerParams(vmem_limit_bytes=8 * 2**20),
        cost_estimate=pl.CostEstimate(
            flops=2 * count * rows * depth * cols,
            bytes_accessed=2 * count * depth * cols,
            transcendentals=0,
        ),
        name=f"project{count}",
    )(att0, att1, *weights)


def projected(att0, att1, weights):
    def sent(value, apart):
        return lax.ppermute(value, "head", [(i, i ^ apart) for i in range(HEAD_PEERS)])

    (distant,) = projection(att0, att1, weights[:1], 1)
    distant_in = sent(distant, 1)
    beside, across, own = projection(att0, att1, weights[1:], 1)
    beside_in = sent(beside, 1)
    across = (across.astype(jnp.float32) + distant_in.astype(jnp.float32)).astype(jnp.bfloat16)
    across_in = sent(across, 2)
    return small_call(
        last_sum_kernel,
        "last_sum",
        [jax.ShapeDtypeStruct(own.shape, own.dtype)],
        (own, beside_in, across_in),
    )[0]


def solution(mesh):
    placed = (P("seq", "head"), P("seq", "head"), P("seq", "head"), P("head", None))
    return jax.shard_map(
        body, mesh=mesh, in_specs=placed, out_specs=P("seq", "head"), check_vma=False
    )
```

```python
import functools
import math

import jax
import jax.numpy as jnp
from jax import lax
from jax.experimental import pallas as pl
from jax.experimental.pallas import tpu as pltpu
from jax.sharding import PartitionSpec as P

HD = 128
SPANS = 64
HEAD_PEERS = 4
ROW = 8
KEYS, VALUES = 4, 3
WEIGHT = 30
LIGHT = pl.CostEstimate(flops=1, bytes_accessed=1, transcendentals=0)
SCALE = math.log2(math.e) / math.sqrt(HD)
LOWEST = -1e30


def scores_of(query, key):
    return lax.dot_general(query, key, (((1,), (1,)), ((), ())), preferred_element_type=jnp.float32)


def with_ones(value):
    return jnp.concatenate([value, jnp.ones_like(value)], axis=1)


def widen(column, times):
    return jnp.concatenate([column] * times, axis=1)


def weights_of(scores, shift):
    return jnp.exp2(scores * SCALE - widen(shift, scores.shape[1] // HD)).astype(jnp.bfloat16)


def inverse(x):
    guess = pl.reciprocal(x, approx=True)
    return guess * (2.0 - x * guess)


def lanes(h):
    return slice(h * HD, (h + 1) * HD)


def near_kernel(q_ref, k_ref, v_ref, pk_ref, pv_ref, state_ref):
    rows = q_ref.shape[0]
    for h in range(q_ref.shape[1] // HD):
        at = lanes(h)
        query = q_ref[:, at]
        s0 = scores_of(query, k_ref[:, at])
        s1 = scores_of(query, pk_ref[:, at])
        top = jnp.maximum(jnp.max(s0, axis=1, keepdims=True), jnp.max(s1, axis=1, keepdims=True))
        top = jnp.broadcast_to(top, (rows, HD))
        shift = top * SCALE
        state_ref[h, :, : 2 * HD] = jnp.dot(
            weights_of(s0, shift), with_ones(v_ref[:, at]), preferred_element_type=jnp.float32
        ) + jnp.dot(
            weights_of(s1, shift), with_ones(pv_ref[:, at]), preferred_element_type=jnp.float32
        )
        state_ref[h, :, 2 * HD :] = top


def far_kernel(heads, held_from, counts, closes, valid_ref, q_ref, state_ref, *refs):
    *arrays, out_ref = refs
    width = q_ref.shape[1] // HD
    rows = q_ref.shape[0]
    groups, at = [], 0
    for direct, relayed in counts:
        groups.append((arrays[at : at + direct], arrays[at + direct : at + direct + relayed]))
        at += direct + relayed

    def part(refs, lane):
        value = refs[0][:, lanes(lane)]
        for ref in refs[1:]:
            value = value + ref[:, lanes(lane)]
        return value

    def key_of(group, h):
        return part(group[0], h) if h < KEYS else part(group[1], h - KEYS)

    def value_of(group, h):
        if h < VALUES:
            return part(group[0], KEYS + h)
        return part(group[1], width - KEYS + h - VALUES)

    for i, h in enumerate(heads):
        query = q_ref[:, lanes(h)]
        old = state_ref[h - held_from, :, 2 * HD :]
        before = state_ref[h - held_from, :, : 2 * HD]
        scores = []
        top = old
        for b, group in enumerate(groups):
            s = scores_of(query, key_of(group, h))
            peak = jnp.broadcast_to(jnp.max(s, axis=1, keepdims=True), (rows, HD))
            top = jnp.maximum(top, jnp.where(valid_ref[b] > 0, peak, LOWEST))
            scores.append(s)
        shift = top * SCALE
        total = before * widen(jnp.exp2(old * SCALE - shift), 2)
        for b, group in enumerate(groups):
            used = jnp.where(valid_ref[b] > 0, shift, -LOWEST)
            total += jnp.dot(
                weights_of(scores[b], used),
                with_ones(value_of(group, h)),
                preferred_element_type=jnp.float32,
            )
        if closes:
            out_ref[:, lanes(i)] = (total[:, :HD] * inverse(total[:, HD:])).astype(out_ref.dtype)
        else:
            out_ref[i, :, : 2 * HD] = total
            out_ref[i, :, 2 * HD :] = top


def pack_kernel(k_ref, v_ref, direct_ref, relayed_ref, direct_stage, relayed_stage, sems):
    keys, values = KEYS * HD, VALUES * HD
    total = k_ref.shape[1]
    moves = []
    for ref, start, wide, out, stage, at in (
        (k_ref, keys, total - keys, relayed_ref, relayed_stage, 0),
        (v_ref, values, total - values, relayed_ref, relayed_stage, total - keys),
        (k_ref, 0, keys, direct_ref, direct_stage, 0),
        (v_ref, 0, values, direct_ref, direct_stage, keys),
    ):
        i, place = len(moves), pl.ds(at, wide)
        moves.append(
            (
                pltpu.make_async_copy(
                    ref.at[:, pl.ds(start, wide)], stage.at[:, place], sems.at[0, i]
                ),
                pltpu.make_async_copy(stage.at[:, place], out.at[:, place], sems.at[1, i]),
            )
        )
    for come, _ in moves:
        come.start()
    for come, go in moves:
        come.wait()
        go.start()
    for _, go in moves:
        go.wait()


def columns_kernel(which_ref, w_ref, *refs):
    *outs, sems = refs
    copies = []
    for i, out in enumerate(outs):
        cols = out.shape[1]
        at = pl.ds(pl.multiple_of(which_ref[i] * cols, cols), cols)
        copies.append(pltpu.make_async_copy(w_ref.at[:, at], out, sems.at[i]))
    for copy in copies:
        copy.start()
    for copy in copies:
        copy.wait()


def project_kernel(att0_ref, att1_ref, *refs):
    half = len(refs) // 2
    weights, outs = (refs[:1], refs[1:]) if len(refs) == 3 else (refs[:half], refs[half:])
    cut = att0_ref.shape[1]
    each = len(outs) // len(weights)
    for i, w_ref in enumerate(weights):
        for j in range(each):
            out_ref = outs[i * each + j]
            rows = out_ref.shape[0]
            at = slice(j * rows, (j + 1) * rows)
            out_ref[...] = (
                jnp.dot(att0_ref[at, :], w_ref[:cut, :], preferred_element_type=jnp.float32)
                + jnp.dot(att1_ref[at, :], w_ref[cut:, :], preferred_element_type=jnp.float32)
            ).astype(out_ref.dtype)


def last_sum_kernel(*refs):
    *parts, out_ref = refs
    out_ref[...] = sum(ref[...].astype(jnp.float32) for ref in parts).astype(out_ref.dtype)


def in_vmem(count):
    return [pl.BlockSpec(memory_space=pltpu.VMEM)] * count


def near_part(q, k, v, pk, pv):
    rows, width = q.shape
    heads = width // HD
    return pl.pallas_call(
        near_kernel,
        out_shape=jax.ShapeDtypeStruct((heads, rows, 3 * HD), jnp.float32),
        in_specs=in_vmem(5),
        out_specs=in_vmem(1)[0],
        compiler_params=pltpu.CompilerParams(vmem_limit_bytes=8 * 2**20),
        cost_estimate=pl.CostEstimate(
            flops=WEIGHT * 12 * heads * rows * rows * HD,
            bytes_accessed=10 * rows * width,
            transcendentals=2 * heads * rows * rows,
        ),
        name="near",
    )(q, k, v, pk, pv)


def far_part(heads, held_from, closes, valid, q, state, blocks):
    rows = q.shape[0]
    arrays = [array for block in blocks for part in block for array in part]
    if closes:
        shape = jax.ShapeDtypeStruct((rows, len(heads) * HD), jnp.bfloat16)
    else:
        shape = jax.ShapeDtypeStruct((len(heads), rows, 3 * HD), jnp.float32)
    counts = [(len(direct), len(relayed)) for direct, relayed in blocks]
    return pl.pallas_call(
        functools.partial(far_kernel, list(heads), held_from, counts, closes),
        out_shape=shape,
        in_specs=[pl.BlockSpec(memory_space=pltpu.SMEM)] + in_vmem(2 + len(arrays)),
        out_specs=in_vmem(1)[0],
        compiler_params=pltpu.CompilerParams(vmem_limit_bytes=8 * 2**20),
        cost_estimate=LIGHT,
        name=f"far{heads[0]}_{len(heads)}",
    )(valid, q, state, *arrays)


def packed(k, v):
    rows, width = k.shape
    direct = (KEYS + VALUES) * HD
    shapes = [(rows, direct), (rows, 2 * width - direct)]
    return pl.pallas_call(
        pack_kernel,
        out_shape=[jax.ShapeDtypeStruct(shape, k.dtype) for shape in shapes],
        in_specs=[pl.BlockSpec(memory_space=pl.ANY)] * 2,
        out_specs=[pl.BlockSpec(memory_space=pl.ANY)] * 2,
        scratch_shapes=[pltpu.VMEM(shape, k.dtype) for shape in shapes]
        + [pltpu.SemaphoreType.DMA((2, 4))],
        compiler_params=pltpu.CompilerParams(vmem_limit_bytes=60 * 2**20),
        cost_estimate=LIGHT,
        name="pack",
    )(k, v)


def seq_pairs(step_of, among=lambda s: True):
    return [
        (s, s + step_of(s)) for s in range(SPANS) if 0 <= s + step_of(s) < SPANS and among(s)
    ]


def mate_step(s):
    return 2 if s // 2 % 2 == 0 else -2


def other_step(s):
    return -mate_step(s)


def is_end(s):
    return s % ROW < 2 or s % ROW >= ROW - 2


MATE = seq_pairs(mate_step)
OTHER = seq_pairs(other_step)
OTHER_IN_ROW = seq_pairs(other_step, lambda s: not is_end(s))
ONWARD = [
    (s + mate_step(s), s + other_step(s))
    for s in range(SPANS)
    if is_end(s) and 0 <= s + other_step(s) < SPANS
]
PAIR = seq_pairs(lambda s: 1 if s % 2 == 0 else -1)
MATE_SHARED = [(s, p) for s, p in PAIR if s % 2 == s // 2 % 2]
OTHER_SHARED = [(s, p) for s, p in PAIR if s % 2 != s // 2 % 2]


def body(queries, key_states, value_states, out_weight):
    place = lax.axis_index("seq")
    chip = place // 2
    mate_chip = chip ^ 1
    other_chip = 2 * chip - mate_chip
    third = jnp.where(place % 2 == 0, chip - 1, chip + 1)

    def inside(c):
        return (c >= 0) & (c < SPANS // 2)

    valid = jnp.stack([inside(mate_chip), inside(other_chip), inside(third)]).astype(jnp.int32)

    pair_key = lax.ppermute(key_states, "seq", PAIR)
    pair_value = lax.ppermute(value_states, "seq", PAIR)
    direct, relayed = packed(key_states, value_states)
    mate1 = lax.ppermute(relayed, "seq", MATE)
    other0 = lax.ppermute(direct, "seq", OTHER)
    direct, relayed, pair_key, pair_value = lax.optimization_barrier(
        (direct, relayed, pair_key, pair_value)
    )
    mate0 = lax.ppermute(direct, "seq", MATE)
    row_other1 = lax.ppermute(relayed, "seq", OTHER_IN_ROW)

    state = near_part(queries, key_states, value_states, pair_key, pair_value)
    mate1, state, out_weight = lax.optimization_barrier((mate1, state, out_weight))
    passed_other1 = lax.ppermute(mate1, "seq", ONWARD)
    z = lax.axis_index("head")
    weights = weight_columns(jnp.stack([z ^ 3, z ^ 1, z ^ 2, z]), out_weight)
    state, *weights = lax.optimization_barrier((state, *weights))

    heads = range(queries.shape[1] // HD)
    soon, later = heads[: min(KEYS, VALUES)], heads[min(KEYS, VALUES) :]
    state, mate0 = lax.optimization_barrier((state, mate0))
    state = far_part(heads, 0, False, valid[:1], queries, state, [[[mate0], [mate1]]])
    state, other0 = lax.optimization_barrier((state, other0))
    state0 = far_part(soon, 0, False, valid[1:2], queries, state, [[[other0], []]])
    passed_other1, state0 = lax.optimization_barrier((passed_other1, state0))
    other1 = row_other1 + passed_other1

    mate_shared1 = lax.ppermute(mate1, "seq", MATE_SHARED)
    mate_shared0 = lax.ppermute(mate0, "seq", MATE_SHARED)
    other_shared0 = lax.ppermute(other0, "seq", OTHER_SHARED)
    other_shared1 = lax.ppermute(other1, "seq", OTHER_SHARED)
    state, mate_shared0, mate_shared1 = lax.optimization_barrier(
        (state, mate_shared0, mate_shared1)
    )
    state1 = far_part(later, 0, False, valid[1:2], queries, state, [[[other0], [other1]]])
    third0, third1 = [mate_shared0, other_shared0], [mate_shared1, other_shared1]
    att0 = far_part(soon, 0, True, valid[2:], queries, state0, [[third0, []]])
    att1 = far_part(later, later[0], True, valid[2:], queries, state1, [[third0, third1]])
    return projected(att0, att1, weights)


def small_call(kernel, name, out_shape, operands, scalars=(), in_hbm=(), sems=0, limit=8 * 2**20):
    return pl.pallas_call(
        kernel,
        out_shape=out_shape,
        in_specs=[pl.BlockSpec(memory_space=pltpu.SMEM)] * len(scalars)
        + [pl.BlockSpec(memory_space=pltpu.HBM)] * len(in_hbm)
        + in_vmem(len(operands)),
        out_specs=in_vmem(len(out_shape)),
        scratch_shapes=[pltpu.SemaphoreType.DMA((sems,))] if sems else [],
        compiler_params=pltpu.CompilerParams(vmem_limit_bytes=limit),
        cost_estimate=LIGHT,
        name=name,
    )(*[x.astype(jnp.int32) for x in scalars], *in_hbm, *operands)


def weight_columns(which, out_weight):
    depth = out_weight.shape[0]
    cols = out_weight.shape[1] // HEAD_PEERS
    return small_call(
        columns_kernel,
        "columns",
        [jax.ShapeDtypeStruct((depth, cols), out_weight.dtype)] * HEAD_PEERS,
        (),
        scalars=(which,),
        in_hbm=(out_weight,),
        sems=HEAD_PEERS,
        limit=48 * 2**20,
    )


def projection(att0, att1, weights, pieces):
    rows = att0.shape[0]
    depth, cols = weights[0].shape
    count = len(weights)
    return pl.pallas_call(
        project_kernel,
        out_shape=[jax.ShapeDtypeStruct((rows // pieces, cols), jnp.bfloat16)] * (count * pieces),
        in_specs=in_vmem(2 + count),
        out_specs=in_vmem(count * pieces),
        compiler_params=pltpu.CompilerParams(vmem_limit_bytes=8 * 2**20),
        cost_estimate=LIGHT,
        name=f"project{count}",
    )(att0, att1, *weights)


def projected(att0, att1, weights):
    def sent(value, apart):
        return lax.ppermute(value, "head", [(i, i ^ apart) for i in range(HEAD_PEERS)])

    (distant,) = projection(att0, att1, weights[:1], 1)
    distant_in = sent(distant, 1)
    beside, across, own = projection(att0, att1, weights[1:], 1)
    beside_in = sent(beside, 1)
    across = (across.astype(jnp.float32) + distant_in.astype(jnp.float32)).astype(jnp.bfloat16)
    across_in = sent(across, 2)
    return small_call(
        last_sum_kernel,
        "last_sum",
        [jax.ShapeDtypeStruct(own.shape, own.dtype)],
        (own, beside_in, across_in),
    )[0]


def solution(mesh):
    placed = (P("seq", "head"), P("seq", "head"), P("seq", "head"), P("head", None))
    return jax.shard_map(
        body, mesh=mesh, in_specs=placed, out_specs=P("seq", "head"), check_vma=False
    )
```

```python
import functools
import math

import jax
import jax.numpy as jnp
from jax import lax
from jax.experimental import pallas as pl
from jax.experimental.pallas import tpu as pltpu
from jax.sharding import PartitionSpec as P

HD = 128
SPANS = 64
HEAD_PEERS = 4
ROW = 8
KEYS, VALUES = 4, 3
WEIGHT = 30
LIGHT = pl.CostEstimate(flops=1, bytes_accessed=1, transcendentals=0)
SCALE = math.log2(math.e) / math.sqrt(HD)
LOWEST = -1e30


def scores_of(query, key):
    return lax.dot_general(query, key, (((1,), (1,)), ((), ())), preferred_element_type=jnp.float32)


def with_ones(value):
    return jnp.concatenate([value, jnp.ones_like(value)], axis=1)


def widen(column, times):
    return jnp.concatenate([column] * times, axis=1)


def weights_of(scores, shift):
    return jnp.exp2(scores * SCALE - widen(shift, scores.shape[1] // HD)).astype(jnp.bfloat16)


def inverse(x):
    guess = pl.reciprocal(x, approx=True)
    return guess * (2.0 - x * guess)


def lanes(h):
    return slice(h * HD, (h + 1) * HD)


def near_kernel(q_ref, k_ref, v_ref, pk_ref, pv_ref, state_ref):
    rows = q_ref.shape[0]
    for h in range(q_ref.shape[1] // HD):
        at = lanes(h)
        query = q_ref[:, at]
        s0 = scores_of(query, k_ref[:, at])
        s1 = scores_of(query, pk_ref[:, at])
        top = jnp.maximum(jnp.max(s0, axis=1, keepdims=True), jnp.max(s1, axis=1, keepdims=True))
        top = jnp.broadcast_to(top, (rows, HD))
        shift = top * SCALE
        state_ref[h, :, : 2 * HD] = jnp.dot(
            weights_of(s0, shift), with_ones(v_ref[:, at]), preferred_element_type=jnp.float32
        ) + jnp.dot(
            weights_of(s1, shift), with_ones(pv_ref[:, at]), preferred_element_type=jnp.float32
        )
        state_ref[h, :, 2 * HD :] = top


def far_kernel(heads, held_from, counts, closes, valid_ref, q_ref, state_ref, *refs):
    *arrays, out_ref = refs
    width = q_ref.shape[1] // HD
    rows = q_ref.shape[0]
    groups, at = [], 0
    for direct, relayed in counts:
        groups.append((arrays[at : at + direct], arrays[at + direct : at + direct + relayed]))
        at += direct + relayed

    def part(refs, lane):
        value = refs[0][:, lanes(lane)]
        for ref in refs[1:]:
            value = value + ref[:, lanes(lane)]
        return value

    def key_of(group, h):
        return part(group[0], h) if h < KEYS else part(group[1], h - KEYS)

    def value_of(group, h):
        if h < VALUES:
            return part(group[0], KEYS + h)
        return part(group[1], width - KEYS + h - VALUES)

    for i, h in enumerate(heads):
        query = q_ref[:, lanes(h)]
        old = state_ref[h - held_from, :, 2 * HD :]
        before = state_ref[h - held_from, :, : 2 * HD]
        scores = []
        top = old
        for b, group in enumerate(groups):
            s = scores_of(query, key_of(group, h))
            peak = jnp.broadcast_to(jnp.max(s, axis=1, keepdims=True), (rows, HD))
            top = jnp.maximum(top, jnp.where(valid_ref[b] > 0, peak, LOWEST))
            scores.append(s)
        shift = top * SCALE
        total = before * widen(jnp.exp2(old * SCALE - shift), 2)
        for b, group in enumerate(groups):
            used = jnp.where(valid_ref[b] > 0, shift, -LOWEST)
            total += jnp.dot(
                weights_of(scores[b], used),
                with_ones(value_of(group, h)),
                preferred_element_type=jnp.float32,
            )
        if closes:
            out_ref[:, lanes(i)] = (total[:, :HD] * inverse(total[:, HD:])).astype(out_ref.dtype)
        else:
            out_ref[i, :, : 2 * HD] = total
            out_ref[i, :, 2 * HD :] = top


def pack_kernel(k_ref, v_ref, direct_ref, relayed_ref, direct_stage, relayed_stage, sems):
    keys, values = KEYS * HD, VALUES * HD
    total = k_ref.shape[1]
    moves = []
    for ref, start, wide, out, stage, at in (
        (k_ref, keys, total - keys, relayed_ref, relayed_stage, 0),
        (v_ref, values, total - values, relayed_ref, relayed_stage, total - keys),
        (k_ref, 0, keys, direct_ref, direct_stage, 0),
        (v_ref, 0, values, direct_ref, direct_stage, keys),
    ):
        i, place = len(moves), pl.ds(at, wide)
        moves.append(
            (
                pltpu.make_async_copy(
                    ref.at[:, pl.ds(start, wide)], stage.at[:, place], sems.at[0, i]
                ),
                pltpu.make_async_copy(stage.at[:, place], out.at[:, place], sems.at[1, i]),
            )
        )
    for come, _ in moves:
        come.start()
    for come, go in moves:
        come.wait()
        go.start()
    for _, go in moves:
        go.wait()


def columns_kernel(which_ref, w_ref, *refs):
    *outs, sems = refs
    copies = []
    for i, out in enumerate(outs):
        cols = out.shape[1]
        at = pl.ds(pl.multiple_of(which_ref[i] * cols, cols), cols)
        copies.append(pltpu.make_async_copy(w_ref.at[:, at], out, sems.at[i]))
    for copy in copies:
        copy.start()
    for copy in copies:
        copy.wait()


def project_kernel(att0_ref, att1_ref, *refs):
    half = len(refs) // 2
    weights, outs = (refs[:1], refs[1:]) if len(refs) == 3 else (refs[:half], refs[half:])
    cut = att0_ref.shape[1]
    each = len(outs) // len(weights)
    for i, w_ref in enumerate(weights):
        for j in range(each):
            out_ref = outs[i * each + j]
            rows = out_ref.shape[0]
            at = slice(j * rows, (j + 1) * rows)
            out_ref[...] = (
                jnp.dot(att0_ref[at, :], w_ref[:cut, :], preferred_element_type=jnp.float32)
                + jnp.dot(att1_ref[at, :], w_ref[cut:, :], preferred_element_type=jnp.float32)
            ).astype(out_ref.dtype)


def last_sum_kernel(*refs):
    *parts, out_ref = refs
    out_ref[...] = sum(ref[...].astype(jnp.float32) for ref in parts).astype(out_ref.dtype)


def in_vmem(count):
    return [pl.BlockSpec(memory_space=pltpu.VMEM)] * count


def near_part(q, k, v, pk, pv):
    rows, width = q.shape
    heads = width // HD
    return pl.pallas_call(
        near_kernel,
        out_shape=jax.ShapeDtypeStruct((heads, rows, 3 * HD), jnp.float32),
        in_specs=in_vmem(5),
        out_specs=in_vmem(1)[0],
        compiler_params=pltpu.CompilerParams(vmem_limit_bytes=8 * 2**20),
        cost_estimate=pl.CostEstimate(
            flops=WEIGHT * 12 * heads * rows * rows * HD,
            bytes_accessed=10 * rows * width,
            transcendentals=2 * heads * rows * rows,
        ),
        name="near",
    )(q, k, v, pk, pv)


def far_part(heads, held_from, closes, valid, q, state, blocks):
    rows = q.shape[0]
    arrays = [array for block in blocks for part in block for array in part]
    if closes:
        shape = jax.ShapeDtypeStruct((rows, len(heads) * HD), jnp.bfloat16)
    else:
        shape = jax.ShapeDtypeStruct((len(heads), rows, 3 * HD), jnp.float32)
    counts = [(len(direct), len(relayed)) for direct, relayed in blocks]
    return pl.pallas_call(
        functools.partial(far_kernel, list(heads), held_from, counts, closes),
        out_shape=shape,
        in_specs=[pl.BlockSpec(memory_space=pltpu.SMEM)] + in_vmem(2 + len(arrays)),
        out_specs=in_vmem(1)[0],
        compiler_params=pltpu.CompilerParams(vmem_limit_bytes=8 * 2**20),
        cost_estimate=LIGHT,
        name=f"far{heads[0]}_{len(heads)}",
    )(valid, q, state, *arrays)


def packed(k, v):
    rows, width = k.shape
    direct = (KEYS + VALUES) * HD
    shapes = [(rows, direct), (rows, 2 * width - direct)]
    return pl.pallas_call(
        pack_kernel,
        out_shape=[jax.ShapeDtypeStruct(shape, k.dtype) for shape in shapes],
        in_specs=[pl.BlockSpec(memory_space=pl.ANY)] * 2,
        out_specs=[pl.BlockSpec(memory_space=pl.ANY)] * 2,
        scratch_shapes=[pltpu.VMEM(shape, k.dtype) for shape in shapes]
        + [pltpu.SemaphoreType.DMA((2, 4))],
        compiler_params=pltpu.CompilerParams(vmem_limit_bytes=60 * 2**20),
        cost_estimate=LIGHT,
        name="pack",
    )(k, v)


def seq_pairs(step_of, among=lambda s: True):
    return [
        (s, s + step_of(s)) for s in range(SPANS) if 0 <= s + step_of(s) < SPANS and among(s)
    ]


def mate_step(s):
    return 2 if s // 2 % 2 == 0 else -2


def other_step(s):
    return -mate_step(s)


def is_end(s):
    return s % ROW < 2 or s % ROW >= ROW - 2


MATE = seq_pairs(mate_step)
OTHER = seq_pairs(other_step)
OTHER_IN_ROW = seq_pairs(other_step, lambda s: not is_end(s))
ONWARD = [
    (s + mate_step(s), s + other_step(s))
    for s in range(SPANS)
    if is_end(s) and 0 <= s + other_step(s) < SPANS
]
PAIR = seq_pairs(lambda s: 1 if s % 2 == 0 else -1)
MATE_SHARED = [(s, p) for s, p in PAIR if s % 2 == s // 2 % 2]
OTHER_SHARED = [(s, p) for s, p in PAIR if s % 2 != s // 2 % 2]


def body(queries, key_states, value_states, out_weight):
    place = lax.axis_index("seq")
    chip = place // 2
    mate_chip = chip ^ 1
    other_chip = 2 * chip - mate_chip
    third = jnp.where(place % 2 == 0, chip - 1, chip + 1)

    def inside(c):
        return (c >= 0) & (c < SPANS // 2)

    valid = jnp.stack([inside(mate_chip), inside(other_chip), inside(third)]).astype(jnp.int32)

    pair_key = lax.ppermute(key_states, "seq", PAIR)
    pair_value = lax.ppermute(value_states, "seq", PAIR)
    direct, relayed = packed(key_states, value_states)
    mate1 = lax.ppermute(relayed, "seq", MATE)
    other0 = lax.ppermute(direct, "seq", OTHER)
    direct, relayed, pair_key, pair_value = lax.optimization_barrier(
        (direct, relayed, pair_key, pair_value)
    )
    mate0 = lax.ppermute(direct, "seq", MATE)
    row_other1 = lax.ppermute(relayed, "seq", OTHER_IN_ROW)

    state = near_part(queries, key_states, value_states, pair_key, pair_value)
    mate1, state, out_weight = lax.optimization_barrier((mate1, state, out_weight))
    passed_other1 = lax.ppermute(mate1, "seq", ONWARD)
    z = lax.axis_index("head")
    weights = weight_columns(jnp.stack([z ^ 3, z ^ 1, z ^ 2, z]), out_weight)
    state, *weights = lax.optimization_barrier((state, *weights))

    heads = range(queries.shape[1] // HD)
    soon, later = heads[: min(KEYS, VALUES)], heads[min(KEYS, VALUES) :]
    state, mate0 = lax.optimization_barrier((state, mate0))
    state = far_part(heads, 0, False, valid[:1], queries, state, [[[mate0], [mate1]]])
    state, other0 = lax.optimization_barrier((state, other0))
    mate_shared1 = lax.ppermute(mate1, "seq", MATE_SHARED)
    mate_shared0 = lax.ppermute(mate0, "seq", MATE_SHARED)
    state, mate_shared1 = lax.optimization_barrier((state, mate_shared1))
    state0 = far_part(soon, 0, False, valid[1:2], queries, state, [[[other0], []]])
    passed_other1, state0 = lax.optimization_barrier((passed_other1, state0))
    other1 = row_other1 + passed_other1
    other_shared0 = lax.ppermute(other0, "seq", OTHER_SHARED)
    other_shared1 = lax.ppermute(other1, "seq", OTHER_SHARED)
    third0, third1 = [mate_shared0, other_shared0], [mate_shared1, other_shared1]
    att0 = far_part(soon, 0, True, valid[2:], queries, state0, [[third0, []]])
    state, att0 = lax.optimization_barrier((state, att0))
    att1 = far_part(
        later, 0, True, valid[1:], queries, state, [[[other0], [other1]], [third0, third1]]
    )
    return projected(att0, att1, weights)


def small_call(kernel, name, out_shape, operands, scalars=(), in_hbm=(), sems=0, limit=8 * 2**20):
    return pl.pallas_call(
        kernel,
        out_shape=out_shape,
        in_specs=[pl.BlockSpec(memory_space=pltpu.SMEM)] * len(scalars)
        + [pl.BlockSpec(memory_space=pltpu.HBM)] * len(in_hbm)
        + in_vmem(len(operands)),
        out_specs=in_vmem(len(out_shape)),
        scratch_shapes=[pltpu.SemaphoreType.DMA((sems,))] if sems else [],
        compiler_params=pltpu.CompilerParams(vmem_limit_bytes=limit),
        cost_estimate=LIGHT,
        name=name,
    )(*[x.astype(jnp.int32) for x in scalars], *in_hbm, *operands)


def weight_columns(which, out_weight):
    depth = out_weight.shape[0]
    cols = out_weight.shape[1] // HEAD_PEERS
    return small_call(
        columns_kernel,
        "columns",
        [jax.ShapeDtypeStruct((depth, cols), out_weight.dtype)] * HEAD_PEERS,
        (),
        scalars=(which,),
        in_hbm=(out_weight,),
        sems=HEAD_PEERS,
        limit=48 * 2**20,
    )


def projection(att0, att1, weights, pieces):
    rows = att0.shape[0]
    depth, cols = weights[0].shape
    count = len(weights)
    return pl.pallas_call(
        project_kernel,
        out_shape=[jax.ShapeDtypeStruct((rows // pieces, cols), jnp.bfloat16)] * (count * pieces),
        in_specs=in_vmem(2 + count),
        out_specs=in_vmem(count * pieces),
        compiler_params=pltpu.CompilerParams(vmem_limit_bytes=8 * 2**20),
        cost_estimate=LIGHT,
        name=f"project{count}",
    )(att0, att1, *weights)


def projected(att0, att1, weights):
    def sent(value, apart):
        return lax.ppermute(value, "head", [(i, i ^ apart) for i in range(HEAD_PEERS)])

    (distant,) = projection(att0, att1, weights[:1], 1)
    distant_in = sent(distant, 1)
    beside, across, own = projection(att0, att1, weights[1:], 1)
    beside_in = sent(beside, 1)
    across = (across.astype(jnp.float32) + distant_in.astype(jnp.float32)).astype(jnp.bfloat16)
    across_in = sent(across, 2)
    return small_call(
        last_sum_kernel,
        "last_sum",
        [jax.ShapeDtypeStruct(own.shape, own.dtype)],
        (own, beside_in, across_in),
    )[0]


def solution(mesh):
    placed = (P("seq", "head"), P("seq", "head"), P("seq", "head"), P("head", None))
    return jax.shard_map(
        body, mesh=mesh, in_specs=placed, out_specs=P("seq", "head"), check_vma=False
    )
```

```python
import functools
import math

import jax
import jax.numpy as jnp
from jax import lax
from jax.experimental import pallas as pl
from jax.experimental.pallas import tpu as pltpu
from jax.sharding import PartitionSpec as P

HD = 128
SPANS = 64
HEAD_PEERS = 4
ROW = 8
KEYS, VALUES = 4, 3
WEIGHT = 30
LIGHT = pl.CostEstimate(flops=1, bytes_accessed=1, transcendentals=0)
SCALE = math.log2(math.e) / math.sqrt(HD)
LOWEST = -1e30


def scores_of(query, key):
    return lax.dot_general(query, key, (((1,), (1,)), ((), ())), preferred_element_type=jnp.float32)


def with_ones(value):
    return jnp.concatenate([value, jnp.ones_like(value)], axis=1)


def widen(column, times):
    return jnp.concatenate([column] * times, axis=1)


def weights_of(scores, shift):
    return jnp.exp2(scores * SCALE - widen(shift, scores.shape[1] // HD)).astype(jnp.bfloat16)


def inverse(x):
    guess = pl.reciprocal(x, approx=True)
    return guess * (2.0 - x * guess)


def lanes(h):
    return slice(h * HD, (h + 1) * HD)


def near_kernel(q_ref, k_ref, v_ref, pk_ref, pv_ref, state_ref):
    rows = q_ref.shape[0]
    for h in range(q_ref.shape[1] // HD):
        at = lanes(h)
        query = q_ref[:, at]
        s0 = scores_of(query, k_ref[:, at])
        s1 = scores_of(query, pk_ref[:, at])
        top = jnp.maximum(jnp.max(s0, axis=1, keepdims=True), jnp.max(s1, axis=1, keepdims=True))
        top = jnp.broadcast_to(top, (rows, HD))
        shift = top * SCALE
        state_ref[h, :, : 2 * HD] = jnp.dot(
            weights_of(s0, shift), with_ones(v_ref[:, at]), preferred_element_type=jnp.float32
        ) + jnp.dot(
            weights_of(s1, shift), with_ones(pv_ref[:, at]), preferred_element_type=jnp.float32
        )
        state_ref[h, :, 2 * HD :] = top


def far_kernel(heads, held_from, counts, closes, valid_ref, q_ref, state_ref, *refs):
    *arrays, out_ref = refs
    width = q_ref.shape[1] // HD
    rows = q_ref.shape[0]
    groups, at = [], 0
    for direct, relayed in counts:
        groups.append((arrays[at : at + direct], arrays[at + direct : at + direct + relayed]))
        at += direct + relayed

    def part(refs, lane):
        value = refs[0][:, lanes(lane)]
        for ref in refs[1:]:
            value = value + ref[:, lanes(lane)]
        return value

    def key_of(group, h):
        return part(group[0], h) if h < KEYS else part(group[1], h - KEYS)

    def value_of(group, h):
        if h < VALUES:
            return part(group[0], KEYS + h)
        return part(group[1], width - KEYS + h - VALUES)

    for i, h in enumerate(heads):
        query = q_ref[:, lanes(h)]
        old = state_ref[h - held_from, :, 2 * HD :]
        before = state_ref[h - held_from, :, : 2 * HD]
        scores = []
        top = old
        for b, group in enumerate(groups):
            s = scores_of(query, key_of(group, h))
            peak = jnp.broadcast_to(jnp.max(s, axis=1, keepdims=True), (rows, HD))
            top = jnp.maximum(top, jnp.where(valid_ref[b] > 0, peak, LOWEST))
            scores.append(s)
        shift = top * SCALE
        total = before * widen(jnp.exp2(old * SCALE - shift), 2)
        for b, group in enumerate(groups):
            used = jnp.where(valid_ref[b] > 0, shift, -LOWEST)
            total += jnp.dot(
                weights_of(scores[b], used),
                with_ones(value_of(group, h)),
                preferred_element_type=jnp.float32,
            )
        if closes:
            out_ref[:, lanes(i)] = (total[:, :HD] * inverse(total[:, HD:])).astype(out_ref.dtype)
        else:
            out_ref[i, :, : 2 * HD] = total
            out_ref[i, :, 2 * HD :] = top


def pack_kernel(k_ref, v_ref, direct_ref, relayed_ref, sems):
    keys, values = KEYS * HD, VALUES * HD
    total = k_ref.shape[1]
    copies = [
        pltpu.make_async_copy(ref.at[:, pl.ds(start, wide)], out.at[:, pl.ds(at, wide)], sems.at[i])
        for i, (ref, start, wide, out, at) in enumerate(
            (
                (k_ref, keys, total - keys, relayed_ref, 0),
                (v_ref, values, total - values, relayed_ref, total - keys),
                (k_ref, 0, keys, direct_ref, 0),
                (v_ref, 0, values, direct_ref, keys),
            )
        )
    ]
    for copy in copies:
        copy.start()
    for copy in copies:
        copy.wait()


def columns_kernel(which_ref, w_ref, *refs):
    *outs, sems = refs
    copies = []
    for i, out in enumerate(outs):
        cols = out.shape[1]
        at = pl.ds(pl.multiple_of(which_ref[i] * cols, cols), cols)
        copies.append(pltpu.make_async_copy(w_ref.at[:, at], out, sems.at[i]))
    for copy in copies:
        copy.start()
    for copy in copies:
        copy.wait()


def project_kernel(att0_ref, att1_ref, *refs):
    half = len(refs) // 2
    weights, outs = (refs[:1], refs[1:]) if len(refs) == 3 else (refs[:half], refs[half:])
    cut = att0_ref.shape[1]
    each = len(outs) // len(weights)
    for i, w_ref in enumerate(weights):
        for j in range(each):
            out_ref = outs[i * each + j]
            rows = out_ref.shape[0]
            at = slice(j * rows, (j + 1) * rows)
            out_ref[...] = (
                jnp.dot(att0_ref[at, :], w_ref[:cut, :], preferred_element_type=jnp.float32)
                + jnp.dot(att1_ref[at, :], w_ref[cut:, :], preferred_element_type=jnp.float32)
            ).astype(out_ref.dtype)


def last_sum_kernel(*refs):
    *parts, out_ref = refs
    out_ref[...] = sum(ref[...].astype(jnp.float32) for ref in parts).astype(out_ref.dtype)


def in_vmem(count):
    return [pl.BlockSpec(memory_space=pltpu.VMEM)] * count


def near_part(q, k, v, pk, pv):
    rows, width = q.shape
    heads = width // HD
    return pl.pallas_call(
        near_kernel,
        out_shape=jax.ShapeDtypeStruct((heads, rows, 3 * HD), jnp.float32),
        in_specs=in_vmem(5),
        out_specs=in_vmem(1)[0],
        compiler_params=pltpu.CompilerParams(vmem_limit_bytes=8 * 2**20),
        cost_estimate=pl.CostEstimate(
            flops=WEIGHT * 12 * heads * rows * rows * HD,
            bytes_accessed=10 * rows * width,
            transcendentals=2 * heads * rows * rows,
        ),
        name="near",
    )(q, k, v, pk, pv)


def far_part(heads, held_from, closes, valid, q, state, blocks):
    rows = q.shape[0]
    arrays = [array for block in blocks for part in block for array in part]
    if closes:
        shape = jax.ShapeDtypeStruct((rows, len(heads) * HD), jnp.bfloat16)
    else:
        shape = jax.ShapeDtypeStruct((len(heads), rows, 3 * HD), jnp.float32)
    counts = [(len(direct), len(relayed)) for direct, relayed in blocks]
    return pl.pallas_call(
        functools.partial(far_kernel, list(heads), held_from, counts, closes),
        out_shape=shape,
        in_specs=[pl.BlockSpec(memory_space=pltpu.SMEM)] + in_vmem(2 + len(arrays)),
        out_specs=in_vmem(1)[0],
        compiler_params=pltpu.CompilerParams(vmem_limit_bytes=8 * 2**20),
        cost_estimate=LIGHT,
        name=f"far{heads[0]}_{len(heads)}",
    )(valid, q, state, *arrays)


def packed(k, v):
    rows, width = k.shape
    direct = (KEYS + VALUES) * HD
    shapes = [(rows, direct), (rows, 2 * width - direct)]
    return pl.pallas_call(
        pack_kernel,
        out_shape=[jax.ShapeDtypeStruct(shape, k.dtype) for shape in shapes],
        in_specs=[pl.BlockSpec(memory_space=pltpu.HBM)] * 2,
        out_specs=in_vmem(2),
        scratch_shapes=[pltpu.SemaphoreType.DMA((4,))],
        compiler_params=pltpu.CompilerParams(vmem_limit_bytes=8 * 2**20),
        cost_estimate=LIGHT,
        name="pack",
    )(*[pltpu.with_memory_space_constraint(x, pltpu.HBM) for x in (k, v)])


def seq_pairs(step_of, among=lambda s: True):
    return [
        (s, s + step_of(s)) for s in range(SPANS) if 0 <= s + step_of(s) < SPANS and among(s)
    ]


def mate_step(s):
    return 2 if s // 2 % 2 == 0 else -2


def other_step(s):
    return -mate_step(s)


def is_end(s):
    return s % ROW < 2 or s % ROW >= ROW - 2


MATE = seq_pairs(mate_step)
OTHER = seq_pairs(other_step)
OTHER_IN_ROW = seq_pairs(other_step, lambda s: not is_end(s))
ONWARD = [
    (s + mate_step(s), s + other_step(s))
    for s in range(SPANS)
    if is_end(s) and 0 <= s + other_step(s) < SPANS
]
PAIR = seq_pairs(lambda s: 1 if s % 2 == 0 else -1)
MATE_SHARED = [(s, p) for s, p in PAIR if s % 2 == s // 2 % 2]
OTHER_SHARED = [(s, p) for s, p in PAIR if s % 2 != s // 2 % 2]


def body(queries, key_states, value_states, out_weight):
    place = lax.axis_index("seq")
    chip = place // 2
    mate_chip = chip ^ 1
    other_chip = 2 * chip - mate_chip
    third = jnp.where(place % 2 == 0, chip - 1, chip + 1)

    def inside(c):
        return (c >= 0) & (c < SPANS // 2)

    valid = jnp.stack([inside(mate_chip), inside(other_chip), inside(third)]).astype(jnp.int32)

    pair_key = lax.ppermute(key_states, "seq", PAIR)
    pair_value = lax.ppermute(value_states, "seq", PAIR)
    direct, relayed = packed(key_states, value_states)
    mate1 = lax.ppermute(relayed, "seq", MATE)
    other0 = lax.ppermute(direct, "seq", OTHER)
    direct, relayed, pair_key, pair_value = lax.optimization_barrier(
        (direct, relayed, pair_key, pair_value)
    )
    mate0 = lax.ppermute(direct, "seq", MATE)
    row_other1 = lax.ppermute(relayed, "seq", OTHER_IN_ROW)

    state = near_part(queries, key_states, value_states, pair_key, pair_value)
    mate1, state, out_weight = lax.optimization_barrier((mate1, state, out_weight))
    passed_other1 = lax.ppermute(mate1, "seq", ONWARD)
    z = lax.axis_index("head")
    weights = weight_columns(jnp.stack([z ^ 3, z ^ 1, z ^ 2, z]), out_weight)
    state, *weights = lax.optimization_barrier((state, *weights))

    heads = range(queries.shape[1] // HD)
    soon, later = heads[: min(KEYS, VALUES)], heads[min(KEYS, VALUES) :]
    state, mate0 = lax.optimization_barrier((state, mate0))
    state = far_part(heads, 0, False, valid[:1], queries, state, [[[mate0], [mate1]]])
    state, other0 = lax.optimization_barrier((state, other0))
    mate_shared1 = lax.ppermute(mate1, "seq", MATE_SHARED)
    mate_shared0 = lax.ppermute(mate0, "seq", MATE_SHARED)
    state, mate_shared1 = lax.optimization_barrier((state, mate_shared1))
    state0 = far_part(soon, 0, False, valid[1:2], queries, state, [[[other0], []]])
    passed_other1, state0 = lax.optimization_barrier((passed_other1, state0))
    other1 = row_other1 + passed_other1
    other_shared0 = lax.ppermute(other0, "seq", OTHER_SHARED)
    other_shared1 = lax.ppermute(other1, "seq", OTHER_SHARED)
    third0, third1 = [mate_shared0, other_shared0], [mate_shared1, other_shared1]
    att0 = far_part(soon, 0, True, valid[2:], queries, state0, [[third0, []]])
    state, att0 = lax.optimization_barrier((state, att0))
    att1 = far_part(
        later, 0, True, valid[1:], queries, state, [[[other0], [other1]], [third0, third1]]
    )
    return projected(att0, att1, weights)


def small_call(kernel, name, out_shape, operands, scalars=(), in_hbm=(), sems=0, limit=8 * 2**20):
    return pl.pallas_call(
        kernel,
        out_shape=out_shape,
        in_specs=[pl.BlockSpec(memory_space=pltpu.SMEM)] * len(scalars)
        + [pl.BlockSpec(memory_space=pltpu.HBM)] * len(in_hbm)
        + in_vmem(len(operands)),
        out_specs=in_vmem(len(out_shape)),
        scratch_shapes=[pltpu.SemaphoreType.DMA((sems,))] if sems else [],
        compiler_params=pltpu.CompilerParams(vmem_limit_bytes=limit),
        cost_estimate=LIGHT,
        name=name,
    )(
        *[x.astype(jnp.int32) for x in scalars],
        *[pltpu.with_memory_space_constraint(x, pltpu.HBM) for x in in_hbm],
        *operands,
    )


def weight_columns(which, out_weight):
    depth = out_weight.shape[0]
    cols = out_weight.shape[1] // HEAD_PEERS
    return small_call(
        columns_kernel,
        "columns",
        [jax.ShapeDtypeStruct((depth, cols), out_weight.dtype)] * HEAD_PEERS,
        (),
        scalars=(which,),
        in_hbm=(out_weight,),
        sems=HEAD_PEERS,
        limit=12 * 2**20,
    )


def projection(att0, att1, weights, pieces):
    rows = att0.shape[0]
    depth, cols = weights[0].shape
    count = len(weights)
    return pl.pallas_call(
        project_kernel,
        out_shape=[jax.ShapeDtypeStruct((rows // pieces, cols), jnp.bfloat16)] * (count * pieces),
        in_specs=in_vmem(2 + count),
        out_specs=in_vmem(count * pieces),
        compiler_params=pltpu.CompilerParams(vmem_limit_bytes=8 * 2**20),
        cost_estimate=LIGHT,
        name=f"project{count}",
    )(att0, att1, *weights)


def projected(att0, att1, weights):
    def sent(value, apart):
        return lax.ppermute(value, "head", [(i, i ^ apart) for i in range(HEAD_PEERS)])

    (distant,) = projection(att0, att1, weights[:1], 1)
    distant_in = sent(distant, 1)
    beside, across, own = projection(att0, att1, weights[1:], 1)
    beside_in = sent(beside, 1)
    across = (across.astype(jnp.float32) + distant_in.astype(jnp.float32)).astype(jnp.bfloat16)
    across_in = sent(across, 2)
    return small_call(
        last_sum_kernel,
        "last_sum",
        [jax.ShapeDtypeStruct(own.shape, own.dtype)],
        (own, beside_in, across_in),
    )[0]


def solution(mesh):
    placed = (P("seq", "head"), P("seq", "head"), P("seq", "head"), P("head", None))
    return jax.shard_map(
        body, mesh=mesh, in_specs=placed, out_specs=P("seq", "head"), check_vma=False
    )
```

```python
import functools
import math

import jax
import jax.numpy as jnp
from jax import lax
from jax.experimental import pallas as pl
from jax.experimental.pallas import tpu as pltpu
from jax.sharding import PartitionSpec as P

HD = 128
SPANS = 64
HEAD_PEERS = 4
ROW = 8
KEYS, VALUES = 4, 3
WEIGHT = 30
LIGHT = pl.CostEstimate(flops=1, bytes_accessed=1, transcendentals=0)
SCALE = math.log2(math.e) / math.sqrt(HD)
LOWEST = -1e30


def scores_of(query, key):
    return lax.dot_general(query, key, (((1,), (1,)), ((), ())), preferred_element_type=jnp.float32)


def with_ones(value):
    return jnp.concatenate([value, jnp.ones_like(value)], axis=1)


def widen(column, times):
    return jnp.concatenate([column] * times, axis=1)


def weights_of(scores, shift):
    return jnp.exp2(scores * SCALE - widen(shift, scores.shape[1] // HD)).astype(jnp.bfloat16)


def inverse(x):
    guess = pl.reciprocal(x, approx=True)
    return guess * (2.0 - x * guess)


def lanes(h):
    return slice(h * HD, (h + 1) * HD)


def near_kernel(q_ref, k_ref, v_ref, pk_ref, pv_ref, state_ref):
    rows = q_ref.shape[0]
    for h in range(q_ref.shape[1] // HD):
        at = lanes(h)
        query = q_ref[:, at]
        s0 = scores_of(query, k_ref[:, at])
        s1 = scores_of(query, pk_ref[:, at])
        top = jnp.maximum(jnp.max(s0, axis=1, keepdims=True), jnp.max(s1, axis=1, keepdims=True))
        top = jnp.broadcast_to(top, (rows, HD))
        shift = top * SCALE
        state_ref[h, :, : 2 * HD] = jnp.dot(
            weights_of(s0, shift), with_ones(v_ref[:, at]), preferred_element_type=jnp.float32
        ) + jnp.dot(
            weights_of(s1, shift), with_ones(pv_ref[:, at]), preferred_element_type=jnp.float32
        )
        state_ref[h, :, 2 * HD :] = top


def far_kernel(heads, held_from, counts, closes, valid_ref, q_ref, state_ref, *refs):
    *arrays, out_ref = refs
    width = q_ref.shape[1] // HD
    rows = q_ref.shape[0]
    groups, at = [], 0
    for direct, relayed in counts:
        groups.append((arrays[at : at + direct], arrays[at + direct : at + direct + relayed]))
        at += direct + relayed

    def part(refs, lane):
        value = refs[0][:, lanes(lane)]
        for ref in refs[1:]:
            value = value + ref[:, lanes(lane)]
        return value

    def key_of(group, h):
        return part(group[0], h) if h < KEYS else part(group[1], h - KEYS)

    def value_of(group, h):
        if h < VALUES:
            return part(group[0], KEYS + h)
        return part(group[1], width - KEYS + h - VALUES)

    for i, h in enumerate(heads):
        query = q_ref[:, lanes(h)]
        old = state_ref[h - held_from, :, 2 * HD :]
        before = state_ref[h - held_from, :, : 2 * HD]
        scores = []
        top = old
        for b, group in enumerate(groups):
            s = scores_of(query, key_of(group, h))
            peak = jnp.broadcast_to(jnp.max(s, axis=1, keepdims=True), (rows, HD))
            top = jnp.maximum(top, jnp.where(valid_ref[b] > 0, peak, LOWEST))
            scores.append(s)
        shift = top * SCALE
        total = before * widen(jnp.exp2(old * SCALE - shift), 2)
        for b, group in enumerate(groups):
            used = jnp.where(valid_ref[b] > 0, shift, -LOWEST)
            total += jnp.dot(
                weights_of(scores[b], used),
                with_ones(value_of(group, h)),
                preferred_element_type=jnp.float32,
            )
        if closes:
            out_ref[:, lanes(i)] = (total[:, :HD] * inverse(total[:, HD:])).astype(out_ref.dtype)
        else:
            out_ref[i, :, : 2 * HD] = total
            out_ref[i, :, 2 * HD :] = top


def last_kernel(heads, counts, valid_ref, q_ref, state_ref, *refs):
    *arrays, att_ref, w_ref, out_ref, term_ref = refs
    far_kernel(heads, 0, counts, True, valid_ref, q_ref, state_ref, *arrays, out_ref)
    cut = att_ref.shape[1]
    term_ref[...] = (
        jnp.dot(att_ref[...], w_ref[:cut, :], preferred_element_type=jnp.float32)
        + jnp.dot(out_ref[...], w_ref[cut:, :], preferred_element_type=jnp.float32)
    ).astype(term_ref.dtype)


def pack_kernel(k_ref, v_ref, direct_ref, relayed_ref, sems):
    keys, values = KEYS * HD, VALUES * HD
    total = k_ref.shape[1]
    copies = [
        pltpu.make_async_copy(ref.at[:, pl.ds(start, wide)], out.at[:, pl.ds(at, wide)], sems.at[i])
        for i, (ref, start, wide, out, at) in enumerate(
            (
                (k_ref, keys, total - keys, relayed_ref, 0),
                (v_ref, values, total - values, relayed_ref, total - keys),
                (k_ref, 0, keys, direct_ref, 0),
                (v_ref, 0, values, direct_ref, keys),
            )
        )
    ]
    for copy in copies:
        copy.start()
    for copy in copies:
        copy.wait()


def columns_kernel(which_ref, w_ref, *refs):
    *outs, sems = refs
    copies = []
    for i, out in enumerate(outs):
        cols = out.shape[1]
        at = pl.ds(pl.multiple_of(which_ref[i] * cols, cols), cols)
        copies.append(pltpu.make_async_copy(w_ref.at[:, at], out, sems.at[i]))
    for copy in copies:
        copy.start()
    for copy in copies:
        copy.wait()


def project_kernel(att0_ref, att1_ref, *refs):
    half = len(refs) // 2
    cut = att0_ref.shape[1]
    for w_ref, out_ref in zip(refs[:half], refs[half:]):
        out_ref[...] = (
            jnp.dot(att0_ref[...], w_ref[:cut, :], preferred_element_type=jnp.float32)
            + jnp.dot(att1_ref[...], w_ref[cut:, :], preferred_element_type=jnp.float32)
        ).astype(out_ref.dtype)


def last_sum_kernel(*refs):
    *parts, out_ref = refs
    out_ref[...] = sum(ref[...].astype(jnp.float32) for ref in parts).astype(out_ref.dtype)


def in_vmem(count):
    return [pl.BlockSpec(memory_space=pltpu.VMEM)] * count


def near_part(q, k, v, pk, pv):
    rows, width = q.shape
    heads = width // HD
    return pl.pallas_call(
        near_kernel,
        out_shape=jax.ShapeDtypeStruct((heads, rows, 3 * HD), jnp.float32),
        in_specs=in_vmem(5),
        out_specs=in_vmem(1)[0],
        compiler_params=pltpu.CompilerParams(vmem_limit_bytes=8 * 2**20),
        cost_estimate=pl.CostEstimate(
            flops=WEIGHT * 12 * heads * rows * rows * HD,
            bytes_accessed=10 * rows * width,
            transcendentals=2 * heads * rows * rows,
        ),
        name="near",
    )(q, k, v, pk, pv)


def far_part(heads, held_from, closes, valid, q, state, blocks):
    rows = q.shape[0]
    arrays = [array for block in blocks for part in block for array in part]
    if closes:
        shape = jax.ShapeDtypeStruct((rows, len(heads) * HD), jnp.bfloat16)
    else:
        shape = jax.ShapeDtypeStruct((len(heads), rows, 3 * HD), jnp.float32)
    counts = [(len(direct), len(relayed)) for direct, relayed in blocks]
    return pl.pallas_call(
        functools.partial(far_kernel, list(heads), held_from, counts, closes),
        out_shape=shape,
        in_specs=[pl.BlockSpec(memory_space=pltpu.SMEM)] + in_vmem(2 + len(arrays)),
        out_specs=in_vmem(1)[0],
        compiler_params=pltpu.CompilerParams(vmem_limit_bytes=8 * 2**20),
        cost_estimate=LIGHT,
        name=f"far{heads[0]}_{len(heads)}",
    )(valid, q, state, *arrays)


def last_part(heads, valid, q, state, blocks, att, weight):
    rows = q.shape[0]
    arrays = [array for block in blocks for part in block for array in part]
    counts = [(len(direct), len(relayed)) for direct, relayed in blocks]
    return pl.pallas_call(
        functools.partial(last_kernel, list(heads), counts),
        out_shape=[
            jax.ShapeDtypeStruct((rows, len(heads) * HD), jnp.bfloat16),
            jax.ShapeDtypeStruct((rows, weight.shape[1]), jnp.bfloat16),
        ],
        in_specs=[pl.BlockSpec(memory_space=pltpu.SMEM)] + in_vmem(4 + len(arrays)),
        out_specs=in_vmem(2),
        compiler_params=pltpu.CompilerParams(vmem_limit_bytes=8 * 2**20),
        cost_estimate=LIGHT,
        name="last",
    )(valid, q, state, *arrays, att, weight)


def packed(k, v):
    rows, width = k.shape
    direct = (KEYS + VALUES) * HD
    shapes = [(rows, direct), (rows, 2 * width - direct)]
    return pl.pallas_call(
        pack_kernel,
        out_shape=[jax.ShapeDtypeStruct(shape, k.dtype) for shape in shapes],
        in_specs=[pl.BlockSpec(memory_space=pltpu.HBM)] * 2,
        out_specs=in_vmem(2),
        scratch_shapes=[pltpu.SemaphoreType.DMA((4,))],
        compiler_params=pltpu.CompilerParams(vmem_limit_bytes=8 * 2**20),
        cost_estimate=LIGHT,
        name="pack",
    )(*[pltpu.with_memory_space_constraint(x, pltpu.HBM) for x in (k, v)])


def seq_pairs(step_of, among=lambda s: True):
    return [
        (s, s + step_of(s)) for s in range(SPANS) if 0 <= s + step_of(s) < SPANS and among(s)
    ]


def mate_step(s):
    return 2 if s // 2 % 2 == 0 else -2


def other_step(s):
    return -mate_step(s)


def is_end(s):
    return s % ROW < 2 or s % ROW >= ROW - 2


MATE = seq_pairs(mate_step)
OTHER = seq_pairs(other_step)
OTHER_IN_ROW = seq_pairs(other_step, lambda s: not is_end(s))
ONWARD = [
    (s + mate_step(s), s + other_step(s))
    for s in range(SPANS)
    if is_end(s) and 0 <= s + other_step(s) < SPANS
]
PAIR = seq_pairs(lambda s: 1 if s % 2 == 0 else -1)
MATE_SHARED = [(s, p) for s, p in PAIR if s % 2 == s // 2 % 2]
OTHER_SHARED = [(s, p) for s, p in PAIR if s % 2 != s // 2 % 2]


def body(queries, key_states, value_states, out_weight):
    place = lax.axis_index("seq")
    chip = place // 2
    mate_chip = chip ^ 1
    other_chip = 2 * chip - mate_chip
    third = jnp.where(place % 2 == 0, chip - 1, chip + 1)

    def inside(c):
        return (c >= 0) & (c < SPANS // 2)

    valid = jnp.stack([inside(mate_chip), inside(other_chip), inside(third)]).astype(jnp.int32)

    pair_key = lax.ppermute(key_states, "seq", PAIR)
    pair_value = lax.ppermute(value_states, "seq", PAIR)
    direct, relayed = packed(key_states, value_states)
    mate1 = lax.ppermute(relayed, "seq", MATE)
    other0 = lax.ppermute(direct, "seq", OTHER)
    direct, relayed, pair_key, pair_value = lax.optimization_barrier(
        (direct, relayed, pair_key, pair_value)
    )
    mate0 = lax.ppermute(direct, "seq", MATE)
    row_other1 = lax.ppermute(relayed, "seq", OTHER_IN_ROW)

    state = near_part(queries, key_states, value_states, pair_key, pair_value)
    mate1, state, out_weight = lax.optimization_barrier((mate1, state, out_weight))
    passed_other1 = lax.ppermute(mate1, "seq", ONWARD)
    z = lax.axis_index("head")
    weights = weight_columns(jnp.stack([z ^ 3, z ^ 1, z ^ 2, z]), out_weight)
    state, *weights = lax.optimization_barrier((state, *weights))

    heads = range(queries.shape[1] // HD)
    soon, later = heads[: min(KEYS, VALUES)], heads[min(KEYS, VALUES) :]
    state, mate0 = lax.optimization_barrier((state, mate0))
    state = far_part(heads, 0, False, valid[:1], queries, state, [[[mate0], [mate1]]])
    state, other0 = lax.optimization_barrier((state, other0))
    mate_shared0 = lax.ppermute(mate0, "seq", MATE_SHARED)
    state0 = far_part(soon, 0, False, valid[1:2], queries, state, [[[other0], []]])
    passed_other1, state0 = lax.optimization_barrier((passed_other1, state0))
    other1 = row_other1 + passed_other1
    to_swap = jnp.where(place % 2 == chip % 2, mate1, other1)
    other_shared0 = lax.ppermute(other0, "seq", OTHER_SHARED)
    swapped1 = lax.ppermute(to_swap, "seq", PAIR)
    third0, third1 = [mate_shared0, other_shared0], [swapped1]
    att0 = far_part(soon, 0, True, valid[2:], queries, state0, [[third0, []]])
    state, att0 = lax.optimization_barrier((state, att0))
    att1, distant = last_part(
        later, valid[1:], queries, state, [[[other0], [other1]], [third0, third1]], att0, weights[0]
    )
    return projected(att0, att1, distant, weights[1:])


def small_call(kernel, name, out_shape, operands, scalars=(), in_hbm=(), sems=0, limit=8 * 2**20):
    return pl.pallas_call(
        kernel,
        out_shape=out_shape,
        in_specs=[pl.BlockSpec(memory_space=pltpu.SMEM)] * len(scalars)
        + [pl.BlockSpec(memory_space=pltpu.HBM)] * len(in_hbm)
        + in_vmem(len(operands)),
        out_specs=in_vmem(len(out_shape)),
        scratch_shapes=[pltpu.SemaphoreType.DMA((sems,))] if sems else [],
        compiler_params=pltpu.CompilerParams(vmem_limit_bytes=limit),
        cost_estimate=LIGHT,
        name=name,
    )(
        *[x.astype(jnp.int32) for x in scalars],
        *[pltpu.with_memory_space_constraint(x, pltpu.HBM) for x in in_hbm],
        *operands,
    )


def weight_columns(which, out_weight):
    depth = out_weight.shape[0]
    cols = out_weight.shape[1] // HEAD_PEERS
    return small_call(
        columns_kernel,
        "columns",
        [jax.ShapeDtypeStruct((depth, cols), out_weight.dtype)] * HEAD_PEERS,
        (),
        scalars=(which,),
        in_hbm=(out_weight,),
        sems=HEAD_PEERS,
        limit=12 * 2**20,
    )


def projection(att0, att1, weights):
    rows, cols, count = att0.shape[0], weights[0].shape[1], len(weights)
    return pl.pallas_call(
        project_kernel,
        out_shape=[jax.ShapeDtypeStruct((rows, cols), jnp.bfloat16)] * count,
        in_specs=in_vmem(2 + count),
        out_specs=in_vmem(count),
        compiler_params=pltpu.CompilerParams(vmem_limit_bytes=8 * 2**20),
        cost_estimate=LIGHT,
        name="project",
    )(att0, att1, *weights)


def projected(att0, att1, distant, weights):
    def sent(value, apart):
        return lax.ppermute(value, "head", [(i, i ^ apart) for i in range(HEAD_PEERS)])

    distant_in = sent(distant, 1)
    beside, across, own = projection(att0, att1, weights)
    beside_in = sent(beside, 1)
    across = (across.astype(jnp.float32) + distant_in.astype(jnp.float32)).astype(jnp.bfloat16)
    across_in = sent(across, 2)
    return small_call(
        last_sum_kernel,
        "last_sum",
        [jax.ShapeDtypeStruct(own.shape, own.dtype)],
        (own, beside_in, across_in),
    )[0]


def solution(mesh):
    placed = (P("seq", "head"), P("seq", "head"), P("seq", "head"), P("head", None))
    return jax.shard_map(
        body, mesh=mesh, in_specs=placed, out_specs=P("seq", "head"), check_vma=False
    )
```

```python
import functools
import math

import jax
import jax.numpy as jnp
from jax import lax
from jax.experimental import pallas as pl
from jax.experimental.pallas import tpu as pltpu
from jax.sharding import PartitionSpec as P

HD = 128
SPANS = 64
HEAD_PEERS = 4
ROW = 8
KEYS, VALUES = 4, 3
WEIGHT = 30
LIGHT = pl.CostEstimate(flops=1, bytes_accessed=2 * 10**6, transcendentals=0)
SCALE = math.log2(math.e) / math.sqrt(HD)
LOWEST = -1e30


def scores_of(query, key):
    return lax.dot_general(query, key, (((1,), (1,)), ((), ())), preferred_element_type=jnp.float32)


def with_ones(value):
    return jnp.concatenate([value, jnp.ones_like(value)], axis=1)


def widen(column, times):
    return jnp.concatenate([column] * times, axis=1)


def weights_of(scores, shift):
    return jnp.exp2(scores * SCALE - widen(shift, scores.shape[1] // HD)).astype(jnp.bfloat16)


def inverse(x):
    guess = pl.reciprocal(x, approx=True)
    return guess * (2.0 - x * guess)


def lanes(h):
    return slice(h * HD, (h + 1) * HD)


def near_kernel(q_ref, k_ref, v_ref, pk_ref, pv_ref, state_ref):
    rows = q_ref.shape[0]
    for h in range(q_ref.shape[1] // HD):
        at = lanes(h)
        query = q_ref[:, at]
        s0 = scores_of(query, k_ref[:, at])
        s1 = scores_of(query, pk_ref[:, at])
        top = jnp.maximum(jnp.max(s0, axis=1, keepdims=True), jnp.max(s1, axis=1, keepdims=True))
        top = jnp.broadcast_to(top, (rows, HD))
        shift = top * SCALE
        state_ref[h, :, : 2 * HD] = jnp.dot(
            weights_of(s0, shift), with_ones(v_ref[:, at]), preferred_element_type=jnp.float32
        ) + jnp.dot(
            weights_of(s1, shift), with_ones(pv_ref[:, at]), preferred_element_type=jnp.float32
        )
        state_ref[h, :, 2 * HD :] = top


def far_kernel(heads, held_from, counts, closes, valid_ref, q_ref, state_ref, *refs):
    *arrays, out_ref = refs
    width = q_ref.shape[1] // HD
    rows = q_ref.shape[0]
    groups, at = [], 0
    for direct, relayed in counts:
        groups.append((arrays[at : at + direct], arrays[at + direct : at + direct + relayed]))
        at += direct + relayed

    def part(refs, lane):
        value = refs[0][:, lanes(lane)]
        for ref in refs[1:]:
            value = value + ref[:, lanes(lane)]
        return value

    def key_of(group, h):
        return part(group[0], h) if h < KEYS else part(group[1], h - KEYS)

    def value_of(group, h):
        if h < VALUES:
            return part(group[0], KEYS + h)
        return part(group[1], width - KEYS + h - VALUES)

    for i, h in enumerate(heads):
        query = q_ref[:, lanes(h)]
        old = state_ref[h - held_from, :, 2 * HD :]
        before = state_ref[h - held_from, :, : 2 * HD]
        scores = []
        top = old
        for b, group in enumerate(groups):
            s = scores_of(query, key_of(group, h))
            peak = jnp.broadcast_to(jnp.max(s, axis=1, keepdims=True), (rows, HD))
            top = jnp.maximum(top, jnp.where(valid_ref[b] > 0, peak, LOWEST))
            scores.append(s)
        shift = top * SCALE
        total = before * widen(jnp.exp2(old * SCALE - shift), 2)
        for b, group in enumerate(groups):
            used = jnp.where(valid_ref[b] > 0, shift, -LOWEST)
            total += jnp.dot(
                weights_of(scores[b], used),
                with_ones(value_of(group, h)),
                preferred_element_type=jnp.float32,
            )
        if closes:
            out_ref[:, lanes(i)] = (total[:, :HD] * inverse(total[:, HD:])).astype(out_ref.dtype)
        else:
            out_ref[i, :, : 2 * HD] = total
            out_ref[i, :, 2 * HD :] = top


def last_kernel(heads, counts, valid_ref, q_ref, state_ref, *refs):
    *arrays, att_ref, w_ref, out_ref, term_ref = refs
    far_kernel(heads, 0, counts, True, valid_ref, q_ref, state_ref, *arrays, out_ref)
    cut = att_ref.shape[1]
    term_ref[...] = (
        jnp.dot(att_ref[...], w_ref[:cut, :], preferred_element_type=jnp.float32)
        + jnp.dot(out_ref[...], w_ref[cut:, :], preferred_element_type=jnp.float32)
    ).astype(term_ref.dtype)


def pack_kernel(k_ref, v_ref, direct_ref, relayed_ref, sems):
    keys, values = KEYS * HD, VALUES * HD
    total = k_ref.shape[1]
    copies = [
        pltpu.make_async_copy(ref.at[:, pl.ds(start, wide)], out.at[:, pl.ds(at, wide)], sems.at[i])
        for i, (ref, start, wide, out, at) in enumerate(
            (
                (k_ref, keys, total - keys, relayed_ref, 0),
                (v_ref, values, total - values, relayed_ref, total - keys),
                (k_ref, 0, keys, direct_ref, 0),
                (v_ref, 0, values, direct_ref, keys),
            )
        )
    ]
    for copy in copies:
        copy.start()
    for copy in copies:
        copy.wait()


def columns_kernel(which_ref, w_ref, *refs):
    *outs, sems = refs
    copies = []
    for i, out in enumerate(outs):
        cols = out.shape[1]
        at = pl.ds(pl.multiple_of(which_ref[i] * cols, cols), cols)
        copies.append(pltpu.make_async_copy(w_ref.at[:, at], out, sems.at[i]))
    for copy in copies:
        copy.start()
    for copy in copies:
        copy.wait()


def project_kernel(att0_ref, att1_ref, *refs):
    half = len(refs) // 2
    cut = att0_ref.shape[1]
    for w_ref, out_ref in zip(refs[:half], refs[half:]):
        out_ref[...] = (
            jnp.dot(att0_ref[...], w_ref[:cut, :], preferred_element_type=jnp.float32)
            + jnp.dot(att1_ref[...], w_ref[cut:, :], preferred_element_type=jnp.float32)
        ).astype(out_ref.dtype)


def last_sum_kernel(*refs):
    *parts, out_ref = refs
    out_ref[...] = sum(ref[...].astype(jnp.float32) for ref in parts).astype(out_ref.dtype)


def in_vmem(count):
    return [pl.BlockSpec(memory_space=pltpu.VMEM)] * count


def near_part(q, k, v, pk, pv):
    rows, width = q.shape
    heads = width // HD
    return pl.pallas_call(
        near_kernel,
        out_shape=jax.ShapeDtypeStruct((heads, rows, 3 * HD), jnp.float32),
        in_specs=in_vmem(5),
        out_specs=in_vmem(1)[0],
        compiler_params=pltpu.CompilerParams(vmem_limit_bytes=8 * 2**20),
        cost_estimate=pl.CostEstimate(
            flops=WEIGHT * 12 * heads * rows * rows * HD,
            bytes_accessed=10 * rows * width,
            transcendentals=2 * heads * rows * rows,
        ),
        name="near",
    )(q, k, v, pk, pv)


def far_part(heads, held_from, closes, valid, q, state, blocks):
    rows = q.shape[0]
    arrays = [array for block in blocks for part in block for array in part]
    if closes:
        shape = jax.ShapeDtypeStruct((rows, len(heads) * HD), jnp.bfloat16)
    else:
        shape = jax.ShapeDtypeStruct((len(heads), rows, 3 * HD), jnp.float32)
    counts = [(len(direct), len(relayed)) for direct, relayed in blocks]
    return pl.pallas_call(
        functools.partial(far_kernel, list(heads), held_from, counts, closes),
        out_shape=shape,
        in_specs=[pl.BlockSpec(memory_space=pltpu.SMEM)] + in_vmem(2 + len(arrays)),
        out_specs=in_vmem(1)[0],
        compiler_params=pltpu.CompilerParams(vmem_limit_bytes=8 * 2**20),
        cost_estimate=LIGHT,
        name=f"far{heads[0]}_{len(heads)}",
    )(valid, q, state, *arrays)


def last_part(heads, valid, q, state, blocks, att, weight):
    rows = q.shape[0]
    arrays = [array for block in blocks for part in block for array in part]
    counts = [(len(direct), len(relayed)) for direct, relayed in blocks]
    return pl.pallas_call(
        functools.partial(last_kernel, list(heads), counts),
        out_shape=[
            jax.ShapeDtypeStruct((rows, len(heads) * HD), jnp.bfloat16),
            jax.ShapeDtypeStruct((rows, weight.shape[1]), jnp.bfloat16),
        ],
        in_specs=[pl.BlockSpec(memory_space=pltpu.SMEM)] + in_vmem(4 + len(arrays)),
        out_specs=in_vmem(2),
        compiler_params=pltpu.CompilerParams(vmem_limit_bytes=8 * 2**20),
        cost_estimate=LIGHT,
        name="last",
    )(valid, q, state, *arrays, att, weight)


def packed(k, v):
    rows, width = k.shape
    direct = (KEYS + VALUES) * HD
    shapes = [(rows, direct), (rows, 2 * width - direct)]
    return pl.pallas_call(
        pack_kernel,
        out_shape=[jax.ShapeDtypeStruct(shape, k.dtype) for shape in shapes],
        in_specs=[pl.BlockSpec(memory_space=pltpu.HBM)] * 2,
        out_specs=in_vmem(2),
        scratch_shapes=[pltpu.SemaphoreType.DMA((4,))],
        compiler_params=pltpu.CompilerParams(vmem_limit_bytes=8 * 2**20),
        cost_estimate=LIGHT,
        name="pack",
    )(*[pltpu.with_memory_space_constraint(x, pltpu.HBM) for x in (k, v)])


def seq_pairs(step_of, among=lambda s: True):
    return [
        (s, s + step_of(s)) for s in range(SPANS) if 0 <= s + step_of(s) < SPANS and among(s)
    ]


def mate_step(s):
    return 2 if s // 2 % 2 == 0 else -2


def other_step(s):
    return -mate_step(s)


def is_end(s):
    return s % ROW < 2 or s % ROW >= ROW - 2


MATE = seq_pairs(mate_step)
OTHER = seq_pairs(other_step)
OTHER_IN_ROW = seq_pairs(other_step, lambda s: not is_end(s))
ONWARD = [
    (s + mate_step(s), s + other_step(s))
    for s in range(SPANS)
    if is_end(s) and 0 <= s + other_step(s) < SPANS
]
PAIR = seq_pairs(lambda s: 1 if s % 2 == 0 else -1)
MATE_SHARED = [(s, p) for s, p in PAIR if s % 2 == s // 2 % 2]
OTHER_SHARED = [(s, p) for s, p in PAIR if s % 2 != s // 2 % 2]


def body(queries, key_states, value_states, out_weight):
    place = lax.axis_index("seq")
    chip = place // 2
    mate_chip = chip ^ 1
    other_chip = 2 * chip - mate_chip
    third = jnp.where(place % 2 == 0, chip - 1, chip + 1)

    def inside(c):
        return (c >= 0) & (c < SPANS // 2)

    valid = jnp.stack([inside(mate_chip), inside(other_chip), inside(third)]).astype(jnp.int32)

    pair_key = lax.ppermute(key_states, "seq", PAIR)
    pair_value = lax.ppermute(value_states, "seq", PAIR)
    direct, relayed = packed(key_states, value_states)
    mate1 = lax.ppermute(relayed, "seq", MATE)
    other0 = lax.ppermute(direct, "seq", OTHER)
    direct, pair_key, pair_value = lax.optimization_barrier((direct, pair_key, pair_value))
    mate0 = lax.ppermute(direct, "seq", MATE)

    state = near_part(queries, key_states, value_states, pair_key, pair_value)
    mate1, state, out_weight, key_states, value_states = lax.optimization_barrier(
        (mate1, state, out_weight, key_states, value_states)
    )
    passed_other1 = lax.ppermute(mate1, "seq", ONWARD)
    again = jnp.concatenate([key_states[:, KEYS * HD :], value_states[:, VALUES * HD :]], axis=1)
    row_other1 = lax.ppermute(again, "seq", OTHER_IN_ROW)
    z = lax.axis_index("head")
    weights = weight_columns(jnp.stack([z ^ 3, z ^ 1, z ^ 2, z]), out_weight)
    state, *weights = lax.optimization_barrier((state, *weights))

    heads = range(queries.shape[1] // HD)
    soon, later = heads[: min(KEYS, VALUES)], heads[min(KEYS, VALUES) :]
    state, mate0 = lax.optimization_barrier((state, mate0))
    state = far_part(heads, 0, False, valid[:1], queries, state, [[[mate0], [mate1]]])
    state, other0 = lax.optimization_barrier((state, other0))
    mate_shared0 = lax.ppermute(mate0, "seq", MATE_SHARED)
    state0 = far_part(soon, 0, False, valid[1:2], queries, state, [[[other0], []]])
    passed_other1, state0 = lax.optimization_barrier((passed_other1, state0))
    other1 = row_other1 + passed_other1
    to_swap = jnp.where(place % 2 == chip % 2, mate1, other1)
    other_shared0 = lax.ppermute(other0, "seq", OTHER_SHARED)
    swapped1 = lax.ppermute(to_swap, "seq", PAIR)
    third0, third1 = [mate_shared0, other_shared0], [swapped1]
    att0 = far_part(soon, 0, True, valid[2:], queries, state0, [[third0, []]])
    state, att0 = lax.optimization_barrier((state, att0))
    att1, distant = last_part(
        later, valid[1:], queries, state, [[[other0], [other1]], [third0, third1]], att0, weights[0]
    )
    return projected(att0, att1, distant, weights[1:])


def small_call(kernel, name, out_shape, operands, scalars=(), in_hbm=(), sems=0, limit=8 * 2**20):
    return pl.pallas_call(
        kernel,
        out_shape=out_shape,
        in_specs=[pl.BlockSpec(memory_space=pltpu.SMEM)] * len(scalars)
        + [pl.BlockSpec(memory_space=pltpu.HBM)] * len(in_hbm)
        + in_vmem(len(operands)),
        out_specs=in_vmem(len(out_shape)),
        scratch_shapes=[pltpu.SemaphoreType.DMA((sems,))] if sems else [],
        compiler_params=pltpu.CompilerParams(vmem_limit_bytes=limit),
        cost_estimate=LIGHT,
        name=name,
    )(
        *[x.astype(jnp.int32) for x in scalars],
        *[pltpu.with_memory_space_constraint(x, pltpu.HBM) for x in in_hbm],
        *operands,
    )


def weight_columns(which, out_weight):
    depth = out_weight.shape[0]
    cols = out_weight.shape[1] // HEAD_PEERS
    return small_call(
        columns_kernel,
        "columns",
        [jax.ShapeDtypeStruct((depth, cols), out_weight.dtype)] * HEAD_PEERS,
        (),
        scalars=(which,),
        in_hbm=(out_weight,),
        sems=HEAD_PEERS,
        limit=12 * 2**20,
    )


def projection(att0, att1, weights):
    rows, cols, count = att0.shape[0], weights[0].shape[1], len(weights)
    return pl.pallas_call(
        project_kernel,
        out_shape=[jax.ShapeDtypeStruct((rows, cols), jnp.bfloat16)] * count,
        in_specs=in_vmem(2 + count),
        out_specs=in_vmem(count),
        compiler_params=pltpu.CompilerParams(vmem_limit_bytes=8 * 2**20),
        cost_estimate=LIGHT,
        name="project",
    )(att0, att1, *weights)


def projected(att0, att1, distant, weights):
    def sent(value, apart):
        return lax.ppermute(value, "head", [(i, i ^ apart) for i in range(HEAD_PEERS)])

    distant_in = sent(distant, 1)
    beside, across, own = projection(att0, att1, weights)
    beside_in = sent(beside, 1)
    across = (across.astype(jnp.float32) + distant_in.astype(jnp.float32)).astype(jnp.bfloat16)
    across_in = sent(across, 2)
    return small_call(
        last_sum_kernel,
        "last_sum",
        [jax.ShapeDtypeStruct(own.shape, own.dtype)],
        (own, beside_in, across_in),
    )[0]


def solution(mesh):
    placed = (P("seq", "head"), P("seq", "head"), P("seq", "head"), P("head", None))
    return jax.shard_map(
        body, mesh=mesh, in_specs=placed, out_specs=P("seq", "head"), check_vma=False
    )
```

```python
import functools
import math

import jax
import jax.numpy as jnp
from jax import lax
from jax.experimental import pallas as pl
from jax.experimental.pallas import tpu as pltpu
from jax.sharding import PartitionSpec as P

HD = 128
SPANS = 64
HEAD_PEERS = 4
ROW = 8
KEYS, VALUES = 4, 3
WEIGHT = 30
LIGHT = pl.CostEstimate(flops=1, bytes_accessed=1, transcendentals=0)
SCALE = math.log2(math.e) / math.sqrt(HD)
LOWEST = -1e30


def scores_of(query, key):
    return lax.dot_general(query, key, (((1,), (1,)), ((), ())), preferred_element_type=jnp.float32)


def with_ones(value):
    return jnp.concatenate([value, jnp.ones_like(value)], axis=1)


def widen(column, times):
    return jnp.concatenate([column] * times, axis=1)


def weights_of(scores, shift):
    return jnp.exp2(scores * SCALE - widen(shift, scores.shape[1] // HD)).astype(jnp.bfloat16)


def inverse(x):
    guess = pl.reciprocal(x, approx=True)
    return guess * (2.0 - x * guess)


def lanes(h):
    return slice(h * HD, (h + 1) * HD)


def near_kernel(q_ref, k_ref, v_ref, pk_ref, pv_ref, state_ref):
    rows = q_ref.shape[0]
    for h in range(q_ref.shape[1] // HD):
        at = lanes(h)
        query = q_ref[:, at]
        s0 = scores_of(query, k_ref[:, at])
        s1 = scores_of(query, pk_ref[:, at])
        top = jnp.maximum(jnp.max(s0, axis=1, keepdims=True), jnp.max(s1, axis=1, keepdims=True))
        top = jnp.broadcast_to(top, (rows, HD))
        shift = top * SCALE
        state_ref[h, :, : 2 * HD] = jnp.dot(
            weights_of(s0, shift), with_ones(v_ref[:, at]), preferred_element_type=jnp.float32
        ) + jnp.dot(
            weights_of(s1, shift), with_ones(pv_ref[:, at]), preferred_element_type=jnp.float32
        )
        state_ref[h, :, 2 * HD :] = top


def far_kernel(heads, held_from, counts, closes, valid_ref, q_ref, state_ref, *refs):
    *arrays, out_ref = refs
    width = q_ref.shape[1] // HD
    rows = q_ref.shape[0]
    groups, at = [], 0
    for direct, relayed in counts:
        groups.append((arrays[at : at + direct], arrays[at + direct : at + direct + relayed]))
        at += direct + relayed

    def part(refs, lane):
        value = refs[0][:, lanes(lane)]
        for ref in refs[1:]:
            value = value + ref[:, lanes(lane)]
        return value

    def key_of(group, h):
        return part(group[0], h) if h < KEYS else part(group[1], h - KEYS)

    def value_of(group, h):
        if h < VALUES:
            return part(group[0], KEYS + h)
        return part(group[1], width - KEYS + h - VALUES)

    for i, h in enumerate(heads):
        query = q_ref[:, lanes(h)]
        old = state_ref[h - held_from, :, 2 * HD :]
        before = state_ref[h - held_from, :, : 2 * HD]
        scores = []
        top = old
        for b, group in enumerate(groups):
            s = scores_of(query, key_of(group, h))
            peak = jnp.broadcast_to(jnp.max(s, axis=1, keepdims=True), (rows, HD))
            top = jnp.maximum(top, jnp.where(valid_ref[b] > 0, peak, LOWEST))
            scores.append(s)
        shift = top * SCALE
        total = before * widen(jnp.exp2(old * SCALE - shift), 2)
        for b, group in enumerate(groups):
            used = jnp.where(valid_ref[b] > 0, shift, -LOWEST)
            total += jnp.dot(
                weights_of(scores[b], used),
                with_ones(value_of(group, h)),
                preferred_element_type=jnp.float32,
            )
        if closes:
            out_ref[:, lanes(i)] = (total[:, :HD] * inverse(total[:, HD:])).astype(out_ref.dtype)
        else:
            out_ref[i, :, : 2 * HD] = total
            out_ref[i, :, 2 * HD :] = top


def last_kernel(heads, counts, valid_ref, q_ref, state_ref, *refs):
    *arrays, att_ref, w_ref, out_ref, term_ref = refs
    far_kernel(heads, 0, counts, True, valid_ref, q_ref, state_ref, *arrays, out_ref)
    cut = att_ref.shape[1]
    term_ref[...] = (
        jnp.dot(att_ref[...], w_ref[:cut, :], preferred_element_type=jnp.float32)
        + jnp.dot(out_ref[...], w_ref[cut:, :], preferred_element_type=jnp.float32)
    ).astype(term_ref.dtype)


def pack_kernel(k_ref, v_ref, direct_ref, relayed_ref, sems):
    keys, values = KEYS * HD, VALUES * HD
    total = k_ref.shape[1]
    copies = [
        pltpu.make_async_copy(ref.at[:, pl.ds(start, wide)], out.at[:, pl.ds(at, wide)], sems.at[i])
        for i, (ref, start, wide, out, at) in enumerate(
            (
                (k_ref, keys, total - keys, relayed_ref, 0),
                (v_ref, values, total - values, relayed_ref, total - keys),
                (k_ref, 0, keys, direct_ref, 0),
                (v_ref, 0, values, direct_ref, keys),
            )
        )
    ]
    for copy in copies:
        copy.start()
    for copy in copies:
        copy.wait()


def columns_kernel(which_ref, w_ref, *refs):
    *outs, sems = refs
    copies = []
    for i, out in enumerate(outs):
        cols = out.shape[1]
        at = pl.ds(pl.multiple_of(which_ref[i] * cols, cols), cols)
        copies.append(pltpu.make_async_copy(w_ref.at[:, at], out, sems.at[i]))
    for copy in copies:
        copy.start()
    for copy in copies:
        copy.wait()


def project_kernel(att0_ref, att1_ref, *refs):
    half = len(refs) // 2
    cut = att0_ref.shape[1]
    for w_ref, out_ref in zip(refs[:half], refs[half:]):
        out_ref[...] = (
            jnp.dot(att0_ref[...], w_ref[:cut, :], preferred_element_type=jnp.float32)
            + jnp.dot(att1_ref[...], w_ref[cut:, :], preferred_element_type=jnp.float32)
        ).astype(out_ref.dtype)


def last_sum_kernel(*refs):
    *parts, out_ref = refs
    out_ref[...] = sum(ref[...].astype(jnp.float32) for ref in parts).astype(out_ref.dtype)


def in_vmem(count):
    return [pl.BlockSpec(memory_space=pltpu.VMEM)] * count


def near_part(q, k, v, pk, pv):
    rows, width = q.shape
    heads = width // HD
    return pl.pallas_call(
        near_kernel,
        out_shape=jax.ShapeDtypeStruct((heads, rows, 3 * HD), jnp.float32),
        in_specs=in_vmem(5),
        out_specs=in_vmem(1)[0],
        compiler_params=pltpu.CompilerParams(vmem_limit_bytes=8 * 2**20),
        cost_estimate=pl.CostEstimate(
            flops=WEIGHT * 12 * heads * rows * rows * HD,
            bytes_accessed=10 * rows * width,
            transcendentals=2 * heads * rows * rows,
        ),
        name="near",
    )(q, k, v, pk, pv)


def far_part(heads, held_from, closes, valid, q, state, blocks):
    rows = q.shape[0]
    arrays = [array for block in blocks for part in block for array in part]
    if closes:
        shape = jax.ShapeDtypeStruct((rows, len(heads) * HD), jnp.bfloat16)
    else:
        shape = jax.ShapeDtypeStruct((len(heads), rows, 3 * HD), jnp.float32)
    counts = [(len(direct), len(relayed)) for direct, relayed in blocks]
    return pl.pallas_call(
        functools.partial(far_kernel, list(heads), held_from, counts, closes),
        out_shape=shape,
        in_specs=[pl.BlockSpec(memory_space=pltpu.SMEM)] + in_vmem(2 + len(arrays)),
        out_specs=in_vmem(1)[0],
        compiler_params=pltpu.CompilerParams(vmem_limit_bytes=8 * 2**20),
        cost_estimate=LIGHT,
        name=f"far{heads[0]}_{len(heads)}",
    )(valid, q, state, *arrays)


def last_part(heads, valid, q, state, blocks, att, weight):
    rows = q.shape[0]
    arrays = [array for block in blocks for part in block for array in part]
    counts = [(len(direct), len(relayed)) for direct, relayed in blocks]
    return pl.pallas_call(
        functools.partial(last_kernel, list(heads), counts),
        out_shape=[
            jax.ShapeDtypeStruct((rows, len(heads) * HD), jnp.bfloat16),
            jax.ShapeDtypeStruct((rows, weight.shape[1]), jnp.bfloat16),
        ],
        in_specs=[pl.BlockSpec(memory_space=pltpu.SMEM)] + in_vmem(4 + len(arrays)),
        out_specs=in_vmem(2),
        compiler_params=pltpu.CompilerParams(vmem_limit_bytes=8 * 2**20),
        cost_estimate=LIGHT,
        name="last",
    )(valid, q, state, *arrays, att, weight)


def packed(k, v):
    rows, width = k.shape
    direct = (KEYS + VALUES) * HD
    shapes = [(rows, direct), (rows, 2 * width - direct)]
    return pl.pallas_call(
        pack_kernel,
        out_shape=[jax.ShapeDtypeStruct(shape, k.dtype) for shape in shapes],
        in_specs=[pl.BlockSpec(memory_space=pltpu.HBM)] * 2,
        out_specs=in_vmem(2),
        scratch_shapes=[pltpu.SemaphoreType.DMA((4,))],
        compiler_params=pltpu.CompilerParams(vmem_limit_bytes=8 * 2**20),
        cost_estimate=LIGHT,
        name="pack",
    )(*[pltpu.with_memory_space_constraint(x, pltpu.HBM) for x in (k, v)])


def seq_pairs(step_of, among=lambda s: True):
    return [
        (s, s + step_of(s)) for s in range(SPANS) if 0 <= s + step_of(s) < SPANS and among(s)
    ]


def mate_step(s):
    return 2 if s // 2 % 2 == 0 else -2


def other_step(s):
    return -mate_step(s)


def is_end(s):
    return s % ROW < 2 or s % ROW >= ROW - 2


MATE = seq_pairs(mate_step)
OTHER = seq_pairs(other_step)
OTHER_IN_ROW = seq_pairs(other_step, lambda s: not is_end(s))
ONWARD = [
    (s + mate_step(s), s + other_step(s))
    for s in range(SPANS)
    if is_end(s) and 0 <= s + other_step(s) < SPANS
]
PAIR = seq_pairs(lambda s: 1 if s % 2 == 0 else -1)
MATE_SHARED = [(s, p) for s, p in PAIR if s % 2 == s // 2 % 2]
OTHER_SHARED = [(s, p) for s, p in PAIR if s % 2 != s // 2 % 2]


def body(queries, key_states, value_states, out_weight):
    place = lax.axis_index("seq")
    chip = place // 2
    mate_chip = chip ^ 1
    other_chip = 2 * chip - mate_chip
    third = jnp.where(place % 2 == 0, chip - 1, chip + 1)

    def inside(c):
        return (c >= 0) & (c < SPANS // 2)

    valid = jnp.stack([inside(mate_chip), inside(other_chip), inside(third)]).astype(jnp.int32)

    pair_key = lax.ppermute(key_states, "seq", PAIR)
    pair_value = lax.ppermute(value_states, "seq", PAIR)
    direct, relayed = packed(key_states, value_states)
    mate1 = lax.ppermute(relayed, "seq", MATE)
    other0 = lax.ppermute(direct, "seq", OTHER)
    direct, pair_key, pair_value = lax.optimization_barrier((direct, pair_key, pair_value))
    mate0 = lax.ppermute(direct, "seq", MATE)

    state = near_part(queries, key_states, value_states, pair_key, pair_value)
    mate1, state, out_weight, key_states, value_states = lax.optimization_barrier(
        (mate1, state, out_weight, key_states, value_states)
    )
    passed_other1 = lax.ppermute(mate1, "seq", ONWARD)
    again = jnp.concatenate([key_states[:, KEYS * HD :], value_states[:, VALUES * HD :]], axis=1)
    row_other1 = lax.ppermute(again, "seq", OTHER_IN_ROW)
    z = lax.axis_index("head")
    weights = weight_columns(jnp.stack([z ^ 3, z ^ 1, z ^ 2, z]), out_weight)
    state, *weights = lax.optimization_barrier((state, *weights))

    heads = range(queries.shape[1] // HD)
    soon, later = heads[: min(KEYS, VALUES)], heads[min(KEYS, VALUES) :]
    state, mate0 = lax.optimization_barrier((state, mate0))
    state = far_part(heads, 0, False, valid[:1], queries, state, [[[mate0], [mate1]]])
    state, other0 = lax.optimization_barrier((state, other0))
    mate_shared0 = lax.ppermute(mate0, "seq", MATE_SHARED)
    state0 = far_part(soon, 0, False, valid[1:2], queries, state, [[[other0], []]])
    passed_other1, state0 = lax.optimization_barrier((passed_other1, state0))
    to_swap = jnp.where(place % 2 == chip % 2, mate1, row_other1 + passed_other1)
    other_shared0 = lax.ppermute(other0, "seq", OTHER_SHARED)
    swapped1 = lax.ppermute(to_swap, "seq", PAIR)
    third0, third1 = [mate_shared0, other_shared0], [swapped1]
    att0 = far_part(soon, 0, True, valid[2:], queries, state0, [[third0, []]])
    state, att0 = lax.optimization_barrier((state, att0))
    att1, distant = last_part(
        later, valid[1:], queries, state, [[[other0], [row_other1, passed_other1]], [third0, third1]], att0, weights[0]
    )
    return projected(att0, att1, distant, weights[1:])


def small_call(kernel, name, out_shape, operands, scalars=(), in_hbm=(), sems=0, limit=8 * 2**20):
    return pl.pallas_call(
        kernel,
        out_shape=out_shape,
        in_specs=[pl.BlockSpec(memory_space=pltpu.SMEM)] * len(scalars)
        + [pl.BlockSpec(memory_space=pltpu.HBM)] * len(in_hbm)
        + in_vmem(len(operands)),
        out_specs=in_vmem(len(out_shape)),
        scratch_shapes=[pltpu.SemaphoreType.DMA((sems,))] if sems else [],
        compiler_params=pltpu.CompilerParams(vmem_limit_bytes=limit),
        cost_estimate=LIGHT,
        name=name,
    )(
        *[x.astype(jnp.int32) for x in scalars],
        *[pltpu.with_memory_space_constraint(x, pltpu.HBM) for x in in_hbm],
        *operands,
    )


def weight_columns(which, out_weight):
    depth = out_weight.shape[0]
    cols = out_weight.shape[1] // HEAD_PEERS
    return small_call(
        columns_kernel,
        "columns",
        [jax.ShapeDtypeStruct((depth, cols), out_weight.dtype)] * HEAD_PEERS,
        (),
        scalars=(which,),
        in_hbm=(out_weight,),
        sems=HEAD_PEERS,
        limit=12 * 2**20,
    )


def projection(att0, att1, weights):
    rows, cols, count = att0.shape[0], weights[0].shape[1], len(weights)
    return pl.pallas_call(
        project_kernel,
        out_shape=[jax.ShapeDtypeStruct((rows, cols), jnp.bfloat16)] * count,
        in_specs=in_vmem(2 + count),
        out_specs=in_vmem(count),
        compiler_params=pltpu.CompilerParams(vmem_limit_bytes=8 * 2**20),
        cost_estimate=LIGHT,
        name="project",
    )(att0, att1, *weights)


def projected(att0, att1, distant, weights):
    def sent(value, apart):
        return lax.ppermute(value, "head", [(i, i ^ apart) for i in range(HEAD_PEERS)])

    distant_in = sent(distant, 1)
    beside, across, own = projection(att0, att1, weights)
    beside_in = sent(beside, 1)
    across = (across.astype(jnp.float32) + distant_in.astype(jnp.float32)).astype(jnp.bfloat16)
    across_in = sent(across, 2)
    return small_call(
        last_sum_kernel,
        "last_sum",
        [jax.ShapeDtypeStruct(own.shape, own.dtype)],
        (own, beside_in, across_in),
    )[0]


def solution(mesh):
    placed = (P("seq", "head"), P("seq", "head"), P("seq", "head"), P("head", None))
    return jax.shard_map(
        body, mesh=mesh, in_specs=placed, out_specs=P("seq", "head"), check_vma=False
    )
```

```python
import functools
import math

import jax
import jax.numpy as jnp
from jax import lax
from jax.experimental import pallas as pl
from jax.experimental.pallas import tpu as pltpu
from jax.sharding import PartitionSpec as P

HD = 128
SPANS = 64
HEAD_PEERS = 4
ROW = 8
KEYS, VALUES = 3, 4
WEIGHT = 30
LIGHT = pl.CostEstimate(flops=1, bytes_accessed=1, transcendentals=0)
SCALE = math.log2(math.e) / math.sqrt(HD)
LOWEST = -1e30


def scores_of(query, key):
    return lax.dot_general(query, key, (((1,), (1,)), ((), ())), preferred_element_type=jnp.float32)


def with_ones(value):
    return jnp.concatenate([value, jnp.ones_like(value)], axis=1)


def widen(column, times):
    return jnp.concatenate([column] * times, axis=1)


def weights_of(scores, shift):
    return jnp.exp2(scores * SCALE - widen(shift, scores.shape[1] // HD)).astype(jnp.bfloat16)


def inverse(x):
    guess = pl.reciprocal(x, approx=True)
    return guess * (2.0 - x * guess)


def lanes(h):
    return slice(h * HD, (h + 1) * HD)


def near_kernel(q_ref, k_ref, v_ref, pk_ref, pv_ref, state_ref):
    rows = q_ref.shape[0]
    for h in range(q_ref.shape[1] // HD):
        at = lanes(h)
        query = q_ref[:, at]
        s0 = scores_of(query, k_ref[:, at])
        s1 = scores_of(query, pk_ref[:, at])
        top = jnp.maximum(jnp.max(s0, axis=1, keepdims=True), jnp.max(s1, axis=1, keepdims=True))
        top = jnp.broadcast_to(top, (rows, HD))
        shift = top * SCALE
        state_ref[h, :, : 2 * HD] = jnp.dot(
            weights_of(s0, shift), with_ones(v_ref[:, at]), preferred_element_type=jnp.float32
        ) + jnp.dot(
            weights_of(s1, shift), with_ones(pv_ref[:, at]), preferred_element_type=jnp.float32
        )
        state_ref[h, :, 2 * HD :] = top


def far_kernel(heads, held_from, counts, closes, valid_ref, q_ref, state_ref, *refs):
    *arrays, out_ref = refs
    width = q_ref.shape[1] // HD
    rows = q_ref.shape[0]
    groups, at = [], 0
    for direct, relayed in counts:
        groups.append((arrays[at : at + direct], arrays[at + direct : at + direct + relayed]))
        at += direct + relayed

    def part(refs, lane):
        value = refs[0][:, lanes(lane)]
        for ref in refs[1:]:
            value = value + ref[:, lanes(lane)]
        return value

    def key_of(group, h):
        return part(group[0], h) if h < KEYS else part(group[1], h - KEYS)

    def value_of(group, h):
        if h < VALUES:
            return part(group[0], KEYS + h)
        return part(group[1], width - KEYS + h - VALUES)

    for i, h in enumerate(heads):
        query = q_ref[:, lanes(h)]
        old = state_ref[h - held_from, :, 2 * HD :]
        before = state_ref[h - held_from, :, : 2 * HD]
        scores = []
        top = old
        for b, group in enumerate(groups):
            s = scores_of(query, key_of(group, h))
            peak = jnp.broadcast_to(jnp.max(s, axis=1, keepdims=True), (rows, HD))
            top = jnp.maximum(top, jnp.where(valid_ref[b] > 0, peak, LOWEST))
            scores.append(s)
        shift = top * SCALE
        total = before * widen(jnp.exp2(old * SCALE - shift), 2)
        for b, group in enumerate(groups):
            used = jnp.where(valid_ref[b] > 0, shift, -LOWEST)
            total += jnp.dot(
                weights_of(scores[b], used),
                with_ones(value_of(group, h)),
                preferred_element_type=jnp.float32,
            )
        if closes:
            out_ref[:, lanes(i)] = (total[:, :HD] * inverse(total[:, HD:])).astype(out_ref.dtype)
        else:
            out_ref[i, :, : 2 * HD] = total
            out_ref[i, :, 2 * HD :] = top


def last_kernel(heads, counts, valid_ref, q_ref, state_ref, *refs):
    *arrays, att_ref, w_ref, out_ref, term_ref = refs
    far_kernel(heads, 0, counts, True, valid_ref, q_ref, state_ref, *arrays, out_ref)
    cut = att_ref.shape[1]
    term_ref[...] = (
        jnp.dot(att_ref[...], w_ref[:cut, :], preferred_element_type=jnp.float32)
        + jnp.dot(out_ref[...], w_ref[cut:, :], preferred_element_type=jnp.float32)
    ).astype(term_ref.dtype)


def pack_kernel(k_ref, v_ref, direct_ref, relayed_ref, sems):
    keys, values = KEYS * HD, VALUES * HD
    total = k_ref.shape[1]
    copies = [
        pltpu.make_async_copy(ref.at[:, pl.ds(start, wide)], out.at[:, pl.ds(at, wide)], sems.at[i])
        for i, (ref, start, wide, out, at) in enumerate(
            (
                (k_ref, keys, total - keys, relayed_ref, 0),
                (v_ref, values, total - values, relayed_ref, total - keys),
                (k_ref, 0, keys, direct_ref, 0),
                (v_ref, 0, values, direct_ref, keys),
            )
        )
    ]
    for copy in copies:
        copy.start()
    for copy in copies:
        copy.wait()


def columns_kernel(which_ref, w_ref, *refs):
    *outs, sems = refs
    copies = []
    for i, out in enumerate(outs):
        cols = out.shape[1]
        at = pl.ds(pl.multiple_of(which_ref[i] * cols, cols), cols)
        copies.append(pltpu.make_async_copy(w_ref.at[:, at], out, sems.at[i]))
    for copy in copies:
        copy.start()
    for copy in copies:
        copy.wait()


def project_kernel(att0_ref, att1_ref, *refs):
    half = len(refs) // 2
    cut = att0_ref.shape[1]
    for w_ref, out_ref in zip(refs[:half], refs[half:]):
        out_ref[...] = (
            jnp.dot(att0_ref[...], w_ref[:cut, :], preferred_element_type=jnp.float32)
            + jnp.dot(att1_ref[...], w_ref[cut:, :], preferred_element_type=jnp.float32)
        ).astype(out_ref.dtype)


def last_sum_kernel(*refs):
    *parts, out_ref = refs
    out_ref[...] = sum(ref[...].astype(jnp.float32) for ref in parts).astype(out_ref.dtype)


def in_vmem(count):
    return [pl.BlockSpec(memory_space=pltpu.VMEM)] * count


def near_part(q, k, v, pk, pv):
    rows, width = q.shape
    heads = width // HD
    return pl.pallas_call(
        near_kernel,
        out_shape=jax.ShapeDtypeStruct((heads, rows, 3 * HD), jnp.float32),
        in_specs=in_vmem(5),
        out_specs=in_vmem(1)[0],
        compiler_params=pltpu.CompilerParams(vmem_limit_bytes=8 * 2**20),
        cost_estimate=pl.CostEstimate(
            flops=WEIGHT * 12 * heads * rows * rows * HD,
            bytes_accessed=10 * rows * width,
            transcendentals=2 * heads * rows * rows,
        ),
        name="near",
    )(q, k, v, pk, pv)


def far_part(heads, held_from, closes, valid, q, state, blocks):
    rows = q.shape[0]
    arrays = [array for block in blocks for part in block for array in part]
    if closes:
        shape = jax.ShapeDtypeStruct((rows, len(heads) * HD), jnp.bfloat16)
    else:
        shape = jax.ShapeDtypeStruct((len(heads), rows, 3 * HD), jnp.float32)
    counts = [(len(direct), len(relayed)) for direct, relayed in blocks]
    return pl.pallas_call(
        functools.partial(far_kernel, list(heads), held_from, counts, closes),
        out_shape=shape,
        in_specs=[pl.BlockSpec(memory_space=pltpu.SMEM)] + in_vmem(2 + len(arrays)),
        out_specs=in_vmem(1)[0],
        compiler_params=pltpu.CompilerParams(vmem_limit_bytes=8 * 2**20),
        cost_estimate=LIGHT,
        name=f"far{heads[0]}_{len(heads)}",
    )(valid, q, state, *arrays)


def last_part(heads, valid, q, state, blocks, att, weight):
    rows = q.shape[0]
    arrays = [array for block in blocks for part in block for array in part]
    counts = [(len(direct), len(relayed)) for direct, relayed in blocks]
    return pl.pallas_call(
        functools.partial(last_kernel, list(heads), counts),
        out_shape=[
            jax.ShapeDtypeStruct((rows, len(heads) * HD), jnp.bfloat16),
            jax.ShapeDtypeStruct((rows, weight.shape[1]), jnp.bfloat16),
        ],
        in_specs=[pl.BlockSpec(memory_space=pltpu.SMEM)] + in_vmem(4 + len(arrays)),
        out_specs=in_vmem(2),
        compiler_params=pltpu.CompilerParams(vmem_limit_bytes=8 * 2**20),
        cost_estimate=LIGHT,
        name="last",
    )(valid, q, state, *arrays, att, weight)


def packed(k, v):
    rows, width = k.shape
    direct = (KEYS + VALUES) * HD
    shapes = [(rows, direct), (rows, 2 * width - direct)]
    return pl.pallas_call(
        pack_kernel,
        out_shape=[jax.ShapeDtypeStruct(shape, k.dtype) for shape in shapes],
        in_specs=[pl.BlockSpec(memory_space=pltpu.HBM)] * 2,
        out_specs=in_vmem(2),
        scratch_shapes=[pltpu.SemaphoreType.DMA((4,))],
        compiler_params=pltpu.CompilerParams(vmem_limit_bytes=8 * 2**20),
        cost_estimate=LIGHT,
        name="pack",
    )(*[pltpu.with_memory_space_constraint(x, pltpu.HBM) for x in (k, v)])


def seq_pairs(step_of, among=lambda s: True):
    return [
        (s, s + step_of(s)) for s in range(SPANS) if 0 <= s + step_of(s) < SPANS and among(s)
    ]


def mate_step(s):
    return 2 if s // 2 % 2 == 0 else -2


def other_step(s):
    return -mate_step(s)


def is_end(s):
    return s % ROW < 2 or s % ROW >= ROW - 2


MATE = seq_pairs(mate_step)
OTHER = seq_pairs(other_step)
OTHER_IN_ROW = seq_pairs(other_step, lambda s: not is_end(s))
ONWARD = [
    (s + mate_step(s), s + other_step(s))
    for s in range(SPANS)
    if is_end(s) and 0 <= s + other_step(s) < SPANS
]
PAIR = seq_pairs(lambda s: 1 if s % 2 == 0 else -1)
MATE_SHARED = [(s, p) for s, p in PAIR if s % 2 == s // 2 % 2]
OTHER_SHARED = [(s, p) for s, p in PAIR if s % 2 != s // 2 % 2]


def body(queries, key_states, value_states, out_weight):
    place = lax.axis_index("seq")
    chip = place // 2
    mate_chip = chip ^ 1
    other_chip = 2 * chip - mate_chip
    third = jnp.where(place % 2 == 0, chip - 1, chip + 1)

    def inside(c):
        return (c >= 0) & (c < SPANS // 2)

    valid = jnp.stack([inside(mate_chip), inside(other_chip), inside(third)]).astype(jnp.int32)

    pair_key = lax.ppermute(key_states, "seq", PAIR)
    pair_value = lax.ppermute(value_states, "seq", PAIR)
    direct, relayed = packed(key_states, value_states)
    mate1 = lax.ppermute(relayed, "seq", MATE)
    other0 = lax.ppermute(direct, "seq", OTHER)
    direct, pair_key, pair_value = lax.optimization_barrier((direct, pair_key, pair_value))
    mate0 = lax.ppermute(direct, "seq", MATE)

    state = near_part(queries, key_states, value_states, pair_key, pair_value)
    mate1, state, out_weight, key_states, value_states = lax.optimization_barrier(
        (mate1, state, out_weight, key_states, value_states)
    )
    passed_other1 = lax.ppermute(mate1, "seq", ONWARD)
    again = jnp.concatenate([key_states[:, KEYS * HD :], value_states[:, VALUES * HD :]], axis=1)
    row_other1 = lax.ppermute(again, "seq", OTHER_IN_ROW)
    z = lax.axis_index("head")
    weights = weight_columns(jnp.stack([z ^ 3, z ^ 1, z ^ 2, z]), out_weight)
    state, *weights = lax.optimization_barrier((state, *weights))

    heads = range(queries.shape[1] // HD)
    soon, later = heads[: min(KEYS, VALUES)], heads[min(KEYS, VALUES) :]
    state, mate0 = lax.optimization_barrier((state, mate0))
    state = far_part(heads, 0, False, valid[:1], queries, state, [[[mate0], [mate1]]])
    state, other0 = lax.optimization_barrier((state, other0))
    mate_shared0 = lax.ppermute(mate0, "seq", MATE_SHARED)
    state0 = far_part(soon, 0, False, valid[1:2], queries, state, [[[other0], []]])
    passed_other1, state0 = lax.optimization_barrier((passed_other1, state0))
    to_swap = jnp.where(place % 2 == chip % 2, mate1, row_other1 + passed_other1)
    other_shared0 = lax.ppermute(other0, "seq", OTHER_SHARED)
    swapped1 = lax.ppermute(to_swap, "seq", PAIR)
    third0, third1 = [mate_shared0, other_shared0], [swapped1]
    att0 = far_part(soon, 0, True, valid[2:], queries, state0, [[third0, []]])
    state, att0 = lax.optimization_barrier((state, att0))
    att1, distant = last_part(
        later, valid[1:], queries, state, [[[other0], [row_other1, passed_other1]], [third0, third1]], att0, weights[0]
    )
    return projected(att0, att1, distant, weights[1:])


def small_call(kernel, name, out_shape, operands, scalars=(), in_hbm=(), sems=0, limit=8 * 2**20):
    return pl.pallas_call(
        kernel,
        out_shape=out_shape,
        in_specs=[pl.BlockSpec(memory_space=pltpu.SMEM)] * len(scalars)
        + [pl.BlockSpec(memory_space=pltpu.HBM)] * len(in_hbm)
        + in_vmem(len(operands)),
        out_specs=in_vmem(len(out_shape)),
        scratch_shapes=[pltpu.SemaphoreType.DMA((sems,))] if sems else [],
        compiler_params=pltpu.CompilerParams(vmem_limit_bytes=limit),
        cost_estimate=LIGHT,
        name=name,
    )(
        *[x.astype(jnp.int32) for x in scalars],
        *[pltpu.with_memory_space_constraint(x, pltpu.HBM) for x in in_hbm],
        *operands,
    )


def weight_columns(which, out_weight):
    depth = out_weight.shape[0]
    cols = out_weight.shape[1] // HEAD_PEERS
    return small_call(
        columns_kernel,
        "columns",
        [jax.ShapeDtypeStruct((depth, cols), out_weight.dtype)] * HEAD_PEERS,
        (),
        scalars=(which,),
        in_hbm=(out_weight,),
        sems=HEAD_PEERS,
        limit=12 * 2**20,
    )


def projection(att0, att1, weights):
    rows, cols, count = att0.shape[0], weights[0].shape[1], len(weights)
    return pl.pallas_call(
        project_kernel,
        out_shape=[jax.ShapeDtypeStruct((rows, cols), jnp.bfloat16)] * count,
        in_specs=in_vmem(2 + count),
        out_specs=in_vmem(count),
        compiler_params=pltpu.CompilerParams(vmem_limit_bytes=8 * 2**20),
        cost_estimate=LIGHT,
        name="project",
    )(att0, att1, *weights)


def projected(att0, att1, distant, weights):
    def sent(value, apart):
        return lax.ppermute(value, "head", [(i, i ^ apart) for i in range(HEAD_PEERS)])

    distant_in = sent(distant, 1)
    beside, across, own = projection(att0, att1, weights)
    beside_in = sent(beside, 1)
    across = (across.astype(jnp.float32) + distant_in.astype(jnp.float32)).astype(jnp.bfloat16)
    across_in = sent(across, 2)
    return small_call(
        last_sum_kernel,
        "last_sum",
        [jax.ShapeDtypeStruct(own.shape, own.dtype)],
        (own, beside_in, across_in),
    )[0]


def solution(mesh):
    placed = (P("seq", "head"), P("seq", "head"), P("seq", "head"), P("head", None))
    return jax.shard_map(
        body, mesh=mesh, in_specs=placed, out_specs=P("seq", "head"), check_vma=False
    )
```
